32 devices in a mesh: dp: 16 (over z, y, x), tensor: 2 (over core).
Axes of the slice: x: 2, y: 2, z: 4, core: 2. Of those that a mesh axis runs over, the one named last changes fastest.
Arguments:
- hidden_in: bfloat16 [32768, 768], P(('dp', 'tensor')), may hold values from -6 to 6
- first_gain: float32 [768], replicated, may hold values from 0.5 to 1.5
- first_shift: float32 [768], replicated, may hold values from -2 to 2
- qkv_weight: bfloat16 [768, 3, 768], P('dp', None, 'tensor'), may hold values from -0.21875 to 0.21875
- qv_bias: float32 [2, 768], P(None, 'tensor'), may hold values from -2 to 2
- out_weight: bfloat16 [768, 768], P('dp', 'tensor'), may hold values from -0.875 to 0.875
- out_bias: float32 [768], replicated, may hold values from -2 to 2
- second_gain: float32 [768], replicated, may hold values from 0.5 to 1.5
- second_shift: float32 [768], replicated, may hold values from -2 to 2
- fc_weight: bfloat16 [768, 3072], P('dp', 'tensor'), may hold values from -0.21875 to 0.21875
- fc_bias: float32 [3072], P('tensor'), may hold values from -2 to 2
- proj_weight: bfloat16 [768, 3072], P('dp', 'tensor'), may hold values from -0.15625 to 0.15625
- proj_bias: float32 [768], replicated, may hold values from -2 to 2
- cotangent: bfloat16 [32768, 768], P(('dp', 'tensor')), may hold values from -6 to 6
Outputs:
- block_out: bfloat16 [32768, 768], P(('dp', 'tensor'))
- grad_hidden: bfloat16 [32768, 768], P(('dp', 'tensor'))
- grad_first_gain: float32 [768], replicated
- grad_first_shift: float32 [768], replicated
- grad_qkv_weight: float32 [768, 3, 768], P('dp', None, 'tensor')
- grad_qv_bias: float32 [2, 768], P(None, 'tensor')
- grad_out_weight: float32 [768, 768], P('dp', 'tensor')
- grad_out_bias: float32 [768], replicated
- grad_second_gain: float32 [768], replicated
- grad_second_shift: float32 [768], replicated
- grad_fc_weight: float32 [768, 3072], P('dp', 'tensor')
- grad_fc_bias: float32 [3072], P('tensor')
- grad_proj_weight: float32 [768, 3072], P('dp', 'tensor')
- grad_proj_bias: float32 [768], replicated
The draws below stay inside these ranges and needn't reach their ends.
All inputs are finite; a program needn't handle non-finite values.
Results may differ from the reference program's by a relative error of at most 0.017.
Values may be sent and summed in bfloat16 or wider, within the bound.
No kernel may reach another device: no remote copies, remote signals or barrier semaphores. Data moves between devices by JAX's collectives and lax.ppermute only.
A program may use at most 320 MiB of HBM per device.

```python
import math
import jax
import jax.numpy as jnp
from jax import lax

D = 768
HEADS = 12
HEAD_DIM = 64
FF = 3072
SEQ_LEN = 2048
TOKENS = 32768


def with_spikes(entries, key, source, target, blocks, factor):
    owner, partner = [(jnp.arange(entries.shape[axis_at]) // (entries.shape[axis_at] // blocks)).reshape([-1 if axis == axis_at else 1 for axis in range(entries.ndim)]) for axis_at in (source, target)]
    chosen = jax.random.permutation(key, blocks)[partner]
    strong = (owner == chosen) | (owner == (partner + blocks // 2) % blocks)
    return jnp.where(strong, factor * entries, entries)


def block_scale(own_key, shape, shards, smallest, high):
    level, own = 1.0, jax.random.fold_in(own_key, 6)
    for axis_at, blocks in shards:
        heights = jnp.exp(jax.random.uniform(jax.random.fold_in(own, axis_at), (blocks,), jnp.float32, smallest / len(shards), high / len(shards)))
        level = level * jnp.repeat(heights, shape[axis_at] // blocks).reshape([-1 if axis == axis_at else 1 for axis in range(len(shape))])
    return level


def gaussian(key, shape, deviation, reach, pieces=(), kind=jnp.bfloat16):
    drawn = deviation * jax.random.normal(key, shape, jnp.float32)
    if pieces:
        drawn = drawn * block_scale(key, shape, pieces, -0.22, 0.18)
    return jnp.clip(drawn, -reach, reach).astype(kind)


def heavy_noise(key, shape, spread, limit, cuts, heavy, held_as=jnp.bfloat16):
    drawn = spread * jax.random.normal(key, shape, jnp.float32)
    if cuts:
        drawn = drawn * block_scale(key, shape, cuts, -0.22, 0.18)
    return jnp.clip(with_spikes(drawn, jax.random.fold_in(key, 3), *heavy), -limit, limit).astype(held_as)


def setup_inputs(seed: int = 0) -> dict:
    seeds = jax.random.split(jax.random.key(seed), 15)
    return {
        "hidden_in": gaussian(seeds[0], (TOKENS, D), 1.0, 6.0, ((0, 32),)),
        "first_gain": jnp.clip(1.0 + 0.1 * jax.random.normal(seeds[1], (D,), jnp.float32), 0.5, 1.5),
        "first_shift": gaussian(seeds[2], (D,), 0.3, 2.0, (), jnp.float32),
        "qkv_weight": gaussian(seeds[3], (D, 3, D), D ** -0.5, 0.21875, ((0, 16), (2, 2))),
        "qv_bias": gaussian(seeds[4], (2, D), 0.3, 2.0, ((1, 2),), jnp.float32),
        "out_weight": gaussian(seeds[5], (D, D), (D // 16) ** -0.5, 0.875, ((0, 16), (1, 2))),
        "out_bias": gaussian(seeds[6], (D,), 0.3, 2.0, (), jnp.float32),
        "second_gain": jnp.clip(1.0 + 0.1 * jax.random.normal(seeds[7], (D,), jnp.float32), 0.5, 1.5),
        "second_shift": gaussian(seeds[8], (D,), 0.3, 2.0, (), jnp.float32),
        "fc_weight": gaussian(seeds[9], (D, FF), D ** -0.5, 0.21875, ((0, 16), (1, 2))),
        "fc_bias": gaussian(seeds[10], (FF,), 0.3, 2.0, ((0, 2),), jnp.float32),
        "proj_weight": gaussian(seeds[11], (D, FF), (FF // 2) ** -0.5, 0.15625, ((0, 16), (1, 2))),
        "proj_bias": gaussian(seeds[12], (D,), 0.3, 2.0, (), jnp.float32),
        "cotangent": heavy_noise(seeds[13], (TOKENS, D), 1.0, 6.0, ((0, 32),), (0, 1, 32, 2.75)),
    }


@jax.custom_vjp
def low(v):
    return lax.optimization_barrier(v.astype(jnp.bfloat16)).astype(jnp.float32)

@jax.custom_vjp
def low_back(v):
    return v

def low_keep(v):
    return (low(v), None)

def low_pass(kept, grad):
    return (grad,)

def back_keep(v):
    return (v, None)

def back_low(kept, grad):
    return (low(grad),)
low.defvjp(low_keep, low_pass)
low_back.defvjp(back_keep, back_low)

def norm_layer(rows_in, gain_vec, shift_vec):
    row_mean = lax.optimization_barrier(jnp.mean(rows_in, axis=-1, keepdims=True))
    centred = rows_in - row_mean
    variance = lax.optimization_barrier(jnp.mean(centred * centred, axis=-1, keepdims=True))
    return centred * lax.rsqrt(variance + 1e-05) * gain_vec + shift_vec

def attend(queries, keys_all, values):
    block_rows = min(512, SEQ_LEN)
    score_scale = 1.0 / math.sqrt(HEAD_DIM)
    key_index = jnp.arange(SEQ_LEN, dtype=jnp.int32)

    def score_block(start):
        query_block = lax.dynamic_slice_in_dim(queries, start, block_rows, 0)
        scores = score_scale * jnp.einsum('qhd,khd->hqk', query_block, keys_all, precision=lax.Precision.HIGHEST)
        scores = low_back(scores)
        row_index = start + jnp.arange(block_rows, dtype=jnp.int32)
        allowed = key_index[None, :] <= row_index[:, None]
        scores = jnp.where(allowed[None], scores, -1e+30)
        probs = jax.nn.softmax(scores, axis=-1)
        return jnp.einsum('hqk,khd->qhd', low(probs), values, precision=lax.Precision.HIGHEST)
    starts = jnp.arange(SEQ_LEN // block_rows, dtype=jnp.int32) * block_rows
    attended = lax.map(jax.checkpoint(score_block), starts)
    return attended.reshape(SEQ_LEN, HEADS * HEAD_DIM)

def sequence(seq_rows, params):
    first_gain, first_shift, qkv_weight, qv_bias, out_weight, out_bias, second_gain, second_shift, fc_weight, fc_bias, proj_weight, proj_bias = params
    highest = lax.Precision.HIGHEST
    normed_first = low(norm_layer(seq_rows, first_gain, first_shift))
    qkv_bias = jnp.stack([qv_bias[0], jnp.zeros_like(qv_bias[0]), qv_bias[1]])
    projected = jnp.einsum('td,dch->tch', normed_first, qkv_weight, precision=highest) + qkv_bias
    projected = low(low_back(projected))
    queries = projected[:, 0].reshape(SEQ_LEN, HEADS, HEAD_DIM)
    keys_all = projected[:, 1].reshape(SEQ_LEN, HEADS, HEAD_DIM)
    values = projected[:, 2].reshape(SEQ_LEN, HEADS, HEAD_DIM)
    heads_out = low(low_back(attend(queries, keys_all, values)))
    attn_out = low_back(jnp.einsum('th,dh->td', heads_out, out_weight, precision=highest) + out_bias)
    middle = seq_rows + attn_out
    normed_second = low(norm_layer(middle, second_gain, second_shift))
    pre_gelu = low_back(jnp.einsum('td,df->tf', normed_second, fc_weight, precision=highest) + fc_bias)
    activated = low(jax.nn.gelu(pre_gelu, approximate=True))
    mlp_out = low_back(jnp.einsum('tf,df->td', activated, proj_weight, precision=highest) + proj_bias)
    return middle + mlp_out

def whole_layer(hidden_rows, params):

    def run_one(seq_rows):
        return sequence(seq_rows, params)
    shaped = hidden_rows.reshape(TOKENS // SEQ_LEN, SEQ_LEN, D)
    return lax.map(jax.checkpoint(run_one), shaped).reshape(TOKENS, D)

def reference(hidden_in, first_gain, first_shift, qkv_weight, qv_bias, out_weight, out_bias, second_gain, second_shift, fc_weight, fc_bias, proj_weight, proj_bias, cotangent):
    params = (first_gain.astype(jnp.float32), first_shift.astype(jnp.float32), qkv_weight.astype(jnp.float32), qv_bias.astype(jnp.float32), out_weight.astype(jnp.float32), out_bias.astype(jnp.float32), second_gain.astype(jnp.float32), second_shift.astype(jnp.float32), fc_weight.astype(jnp.float32), fc_bias.astype(jnp.float32), proj_weight.astype(jnp.float32), proj_bias.astype(jnp.float32))
    result, pullback = jax.vjp(whole_layer, hidden_in.astype(jnp.float32), params)
    grad_rows, gradients = pullback(cotangent.astype(jnp.float32))
    return (result.astype(jnp.bfloat16), grad_rows.astype(jnp.bfloat16), gradients[0], gradients[1], gradients[2], gradients[3], gradients[4], gradients[5], gradients[6], gradients[7], gradients[8], gradients[9], gradients[10], gradients[11])
```

```python
import functools
import math

import jax
import jax.numpy as jnp
from jax import lax
from jax.experimental import pallas as pl
from jax.experimental.pallas import tpu as pltpu
from jax.sharding import PartitionSpec as P

HEAD_DIM = 64
SEQ_LEN = 2048
PAIR = 2 * HEAD_DIM
F32 = jnp.float32
BF16 = jnp.bfloat16
VMEM_BYTES = 56 * 1024 * 1024
MASKED = -1e30


def norm_layer(rows_in, gain_vec, shift_vec):
    row_mean = jnp.mean(rows_in, axis=-1, keepdims=True)
    centred = rows_in - row_mean
    variance = jnp.mean(centred * centred, axis=-1, keepdims=True)
    return centred * lax.rsqrt(variance + 1e-05) * gain_vec + shift_vec


def gelu_tanh(pre_values):
    return jax.nn.gelu(pre_values, approximate=True)


def dot(left, right, left_axis=1, right_axis=0):
    return lax.dot_general(
        left, right, (((left_axis,), (right_axis,)), ((), ())), preferred_element_type=F32
    )


def forward_kernel(qkv_ref, out_ref, lse_ref, *, rows):
    lane = lax.broadcasted_iota(jnp.int32, (1, PAIR), 1)
    mine = [lane < HEAD_DIM, lane >= HEAD_DIM]
    causal = lax.broadcasted_iota(jnp.int32, (rows, rows), 1) <= lax.broadcasted_iota(
        jnp.int32, (rows, rows), 0
    )
    zero = jnp.zeros((), BF16)
    one = jnp.ones((), BF16)
    scale = jnp.asarray(1.0 / math.sqrt(HEAD_DIM), BF16)
    keys = qkv_ref[:, PAIR : 2 * PAIR]
    values = qkv_ref[:, 2 * PAIR :]
    values_one = [jnp.where(lanes, values, one) for lanes in mine]
    for block in range(SEQ_LEN // rows):
        start = block * rows
        here = pl.ds(start, rows)
        queries = qkv_ref[here, :PAIR] * scale
        halves = []
        for head in range(2):
            query = jnp.where(mine[head], queries, zero)
            near = jnp.where(causal, dot(query, keys[start : start + rows], 1, 1), MASKED)
            top = jnp.max(near, axis=1, keepdims=True)
            if block:
                far = dot(query, keys[:start], 1, 1)
                top = jnp.maximum(top, jnp.max(far, axis=1, keepdims=True))
                far = jnp.exp(far - top).astype(BF16)
            near = jnp.exp(near - top).astype(BF16)
            weighted = dot(near, values_one[head][start : start + rows])
            if block:
                weighted = weighted + dot(far, values_one[head][:start])
            total = pltpu.roll(weighted, HEAD_DIM, 1)
            halves.append(weighted / total)
            lse = top + jnp.log(jnp.where(mine[head], total, weighted))
            lse_ref[head : head + 1, here] = jnp.transpose(lse)[0:1]
        out_ref[here, :] = jnp.where(mine[0], halves[0], halves[1]).astype(BF16)


def backward_kernel(qkv_ref, grad_ref, out_ref, lse_ref, result_ref, dq_ref, *, rows):
    lane = lax.broadcasted_iota(jnp.int32, (1, PAIR), 1)
    mine = [lane < HEAD_DIM, lane >= HEAD_DIM]
    causal = lax.broadcasted_iota(jnp.int32, (rows, rows), 0) <= lax.broadcasted_iota(
        jnp.int32, (rows, rows), 1
    )
    zero = jnp.zeros((), BF16)
    scale = jnp.asarray(1.0 / math.sqrt(HEAD_DIM), BF16)
    grad = grad_ref[...]
    queries = [jnp.where(lanes, qkv_ref[:, :PAIR], zero) * scale for lanes in mine]
    grads = [jnp.where(lanes, grad, zero) for lanes in mine]
    product = jnp.transpose(grad.astype(F32) * out_ref[...].astype(F32))
    delta = [
        jnp.sum(product[:HEAD_DIM], axis=0, keepdims=True),
        jnp.sum(product[HEAD_DIM:], axis=0, keepdims=True),
    ]
    for block in range(SEQ_LEN // rows):
        start = block * rows
        here = pl.ds(start, rows)
        keys = qkv_ref[here, PAIR : 2 * PAIR]
        values = qkv_ref[here, 2 * PAIR :]
        keys_turned = jnp.transpose(keys * scale)
        key_grad = jnp.zeros((rows, PAIR), F32)
        value_grad = jnp.zeros((rows, PAIR), F32)
        for head in range(2):
            part = slice(HEAD_DIM * head, HEAD_DIM * (head + 1))
            for low, high in ((start, start + rows), (start + rows, SEQ_LEN)):
                if low == high:
                    continue
                scores = dot(keys, queries[head][low:high], 1, 1)
                if low == start:
                    scores = jnp.where(causal, scores, MASKED)
                probs = jnp.exp(scores - lse_ref[head : head + 1, low:high])
                grad_probs = dot(values, grads[head][low:high], 1, 1)
                grad_scores = (probs * (grad_probs - delta[head][:, low:high])).astype(BF16)
                value_grad = value_grad + dot(probs.astype(BF16), grads[head][low:high])
                key_grad = key_grad + dot(grad_scores, queries[head][low:high])
                turned = dot(keys_turned[part], grad_scores)
                if block == 0:
                    dq_ref[part, low:high] = turned
                else:
                    dq_ref[part, low:high] += turned
        result_ref[here, PAIR : 2 * PAIR] = key_grad.astype(BF16)
        result_ref[here, 2 * PAIR :] = value_grad.astype(BF16)
    result_ref[:, :PAIR] = jnp.transpose(dq_ref[...]).astype(BF16)


def attend_forward(projected):
    tokens, width = projected.shape
    pairs = width // (3 * PAIR)
    seqs = tokens // SEQ_LEN
    return pl.pallas_call(
        functools.partial(forward_kernel, rows=512),
        grid=(seqs, pairs),
        in_specs=[pl.BlockSpec((SEQ_LEN, 3 * PAIR), lambda s, p: (s, p))],
        out_specs=[
            pl.BlockSpec((SEQ_LEN, PAIR), lambda s, p: (s, p)),
            pl.BlockSpec((None, None, 2, SEQ_LEN), lambda s, p: (s, p, 0, 0)),
        ],
        out_shape=[
            jax.ShapeDtypeStruct((tokens, pairs * PAIR), BF16),
            jax.ShapeDtypeStruct((seqs, pairs, 2, SEQ_LEN), F32),
        ],
        compiler_params=pltpu.CompilerParams(vmem_limit_bytes=VMEM_BYTES),
        cost_estimate=pl.CostEstimate(
            flops=seqs * pairs * 8 * 10**9, bytes_accessed=10 * 2**20, transcendentals=10**7
        ),
        name="attend_forward",
    )(projected)


def attend_backward(projected, grad_heads, heads_flat, lse):
    tokens, width = projected.shape
    pairs = width // (3 * PAIR)
    seqs = tokens // SEQ_LEN
    wide = pl.BlockSpec((SEQ_LEN, 3 * PAIR), lambda s, p: (s, p))
    narrow = pl.BlockSpec((SEQ_LEN, PAIR), lambda s, p: (s, p))
    return pl.pallas_call(
        functools.partial(backward_kernel, rows=256),
        grid=(seqs, pairs),
        in_specs=[
            wide,
            narrow,
            narrow,
            pl.BlockSpec((None, None, 2, SEQ_LEN), lambda s, p: (s, p, 0, 0)),
        ],
        out_specs=wide,
        out_shape=jax.ShapeDtypeStruct((tokens, width), BF16),
        scratch_shapes=[pltpu.VMEM((PAIR, SEQ_LEN), F32)],
        compiler_params=pltpu.CompilerParams(vmem_limit_bytes=VMEM_BYTES),
        cost_estimate=pl.CostEstimate(
            flops=seqs * pairs * 15 * 10**9, bytes_accessed=16 * 2**20, transcendentals=10**7
        ),
        name="attend_backward",
    )(projected, grad_heads, heads_flat, lse)


def bits_of(count):
    return count.bit_length() - 1


def exchange(block, bit):
    count = lax.axis_size("dp")
    return lax.ppermute(block, "dp", [(i, i ^ (1 << bit)) for i in range(count)])


def swap(block):
    count = lax.axis_size("tensor")
    return lax.ppermute(block, "tensor", [(i, count - 1 - i) for i in range(count)])


def bit_order(first):
    bits = bits_of(lax.axis_size("dp"))
    return (first, 1 - first) + tuple(range(2, bits))


def gather_rows(shard, order):
    held = shard[None]
    for bit in order[:-1]:
        held = jnp.concatenate([held, exchange(held, bit)], axis=0)
    return held, exchange(held, order[-1])


def places(order):
    count = lax.axis_size("dp")
    apart = jnp.arange(count, dtype=jnp.int32) ^ lax.axis_index("dp").astype(jnp.int32)
    found = jnp.zeros_like(apart)
    for step, bit in enumerate(order):
        found = found | (((apart >> bit) & 1) << step)
    return found


def arrange_kernel(place_ref, *refs, splits):
    count = pl.num_programs(0)
    owner = pl.program_id(0)
    sources = refs[: 2 * len(splits)]
    results = refs[2 * len(splits) :]
    for number, pieces in enumerate(splits):
        late = place_ref[number * count + owner] >= count // 2
        block = jnp.where(late, sources[2 * number + 1][...], sources[2 * number][...])
        start = 0
        for target, offset, width in pieces:
            results[target][:, :, offset : offset + width] = block[:, :, start : start + width]
            start += width


def arrange(halves, orders, splits, widths):
    count = lax.axis_size("dp")
    half = count // 2
    rows = halves[0][0].shape[1]
    table = jnp.concatenate([places(order) for order in orders])

    def source_spec(number, width):
        return pl.BlockSpec(
            (1, rows, width), lambda i, table: (table[number * count + i] % half, 0, 0)
        )

    operands, in_specs = [], []
    for number, pair in enumerate(halves):
        for part in pair:
            operands.append(part)
            in_specs.append(source_spec(number, part.shape[2]))
    results = pl.pallas_call(
        functools.partial(arrange_kernel, splits=splits),
        grid_spec=pltpu.PrefetchScalarGridSpec(
            num_scalar_prefetch=1,
            grid=(count,),
            in_specs=in_specs,
            out_specs=[pl.BlockSpec((1, rows, w), lambda i, table: (i, 0, 0)) for w in widths],
        ),
        out_shape=[jax.ShapeDtypeStruct((count, rows, w), BF16) for w in widths],
        compiler_params=pltpu.CompilerParams(vmem_limit_bytes=VMEM_BYTES),
        cost_estimate=pl.CostEstimate(
            flops=0, bytes_accessed=3 * 2 * count * rows * sum(widths), transcendentals=0
        ),
        name="arrange",
    )(table, *operands)
    return [block.reshape(count * rows, -1) for block in results]


def scatter_sum(whole, order):
    count = lax.axis_size("dp")
    bits = bits_of(count)
    me = lax.axis_index("dp")
    held = whole.reshape((2,) * bits + (whole.shape[0] // count, whole.shape[1]))
    left = list(range(bits - 1, -1, -1))
    for bit in order:
        axis = left.index(bit)
        left.remove(bit)
        own = (me >> bit) & 1
        away = lax.dynamic_index_in_dim(held, 1 - own, axis, keepdims=False)
        kept = lax.dynamic_index_in_dim(held, own, axis, keepdims=False)
        held = kept + exchange(away.astype(BF16), bit).astype(F32)
    return held


def sum_vectors(vector, both):
    for bit in range(bits_of(lax.axis_size("dp"))):
        vector = vector + exchange(vector, bit)
    return jnp.concatenate([vector[:both] + swap(vector[:both]), vector[both:]])


def per_device(
    hidden_in,
    first_gain,
    first_shift,
    qkv_weight,
    qv_bias,
    out_weight,
    out_bias,
    second_gain,
    second_shift,
    fc_weight,
    fc_bias,
    proj_weight,
    proj_bias,
    cotangent,
):
    tensor_pos = lax.axis_index("tensor")
    half = hidden_in.shape[0]
    width = hidden_in.shape[1]
    shard_rows = qkv_weight.shape[0]
    head_width = qkv_weight.shape[2]
    pairs = head_width // PAIR
    x_last, y_last = bit_order(0)[::-1], bit_order(1)[::-1]
    x_first, y_first = bit_order(0), bit_order(1)

    def in_order(own, other):
        return jnp.where(
            tensor_pos == 0,
            jnp.concatenate([own, other], axis=0),
            jnp.concatenate([other, own], axis=0),
        )

    def split_rows(whole):
        own = lax.dynamic_slice_in_dim(whole, tensor_pos * half, half, 0)
        other = lax.dynamic_slice_in_dim(whole, (1 - tensor_pos) * half, half, 0)
        return own, other

    qkv_cols = (
        qkv_weight.reshape(shard_rows, 3, pairs, PAIR)
        .swapaxes(1, 2)
        .reshape(shard_rows, 3 * head_width)
    )
    early = 2 * head_width
    first_a = gather_rows(qkv_cols[:, :early], x_last)
    first_b = gather_rows(jnp.concatenate([qkv_cols[:, early:], out_weight], axis=1), y_last)

    rows_first = hidden_in.astype(F32)
    normed_piece, first_back = jax.vjp(norm_layer, rows_first, first_gain, first_shift)
    normed_piece = normed_piece.astype(BF16)
    normed_first = in_order(normed_piece, swap(normed_piece))
    cot_other = swap(cotangent)

    full_qkv, full_out = arrange(
        [first_a, first_b],
        [x_last, y_last],
        (((0, 0, early),), ((0, early, head_width), (1, 0, head_width))),
        (3 * head_width, head_width),
    )
    fc_own, proj_own, _ = lax.optimization_barrier((fc_weight, proj_weight, first_a[1][:1, :1, :1]))
    second_a = gather_rows(fc_own, x_last)
    second_b = gather_rows(proj_own, y_last)

    bias_parts = jnp.stack([qv_bias[0], jnp.zeros_like(qv_bias[0]), qv_bias[1]])
    bias_cols = bias_parts.reshape(3, pairs, PAIR).swapaxes(0, 1).reshape(3 * head_width)
    projected = (dot(normed_first, full_qkv) + bias_cols).astype(BF16)
    heads_flat, lse = attend_forward(projected)
    heads_own, heads_other = split_rows(heads_flat)
    attn_other = swap(dot(heads_other, full_out, 1, 1).astype(BF16))
    middle = rows_first + (dot(heads_own, full_out, 1, 1) + attn_other.astype(F32)) + out_bias

    normed_mid, second_back = jax.vjp(norm_layer, middle, second_gain, second_shift)
    normed_own = normed_mid.astype(BF16)
    normed_other = swap(normed_own)
    full_fc, full_proj = arrange(
        [second_a, second_b],
        [x_last, y_last],
        (((0, 0, fc_weight.shape[1]),), ((1, 0, fc_weight.shape[1]),)),
        (fc_weight.shape[1], fc_weight.shape[1]),
    )

    def feed_forward(normed, cot):
        pre_gelu = dot(normed, full_fc) + fc_bias
        activated, gelu_back = jax.vjp(gelu_tanh, pre_gelu)
        activated = activated.astype(BF16)
        terms = dot(activated, full_proj, 1, 1)
        grad_pre = gelu_back(dot(cot, full_proj))[0].astype(BF16)
        back = dot(grad_pre, full_fc, 1, 1)
        return activated, terms, grad_pre, back

    act_other, terms_other, pre_other, back_other = feed_forward(normed_other, cot_other)
    terms_other = swap(terms_other.astype(BF16))
    back_other = swap(back_other.astype(BF16))
    act_own, terms_own, pre_own, back_own = feed_forward(normed_own, cotangent)
    block_out = (middle + (terms_own + terms_other.astype(F32)) + proj_bias).astype(BF16)
    back_second = back_own + back_other.astype(F32)

    grad_top = cotangent.astype(F32)
    mid_part, grad_gain_two, grad_shift_two = second_back(back_second)
    grad_middle = grad_top + mid_part
    grad_attn = grad_middle.astype(BF16)
    grad_attn_full = in_order(grad_attn, swap(grad_attn))

    grad_proj = dot(cotangent, act_own, 0, 0) + dot(cot_other, act_other, 0, 0)
    grad_fc = dot(normed_own, pre_own, 0, 0) + dot(normed_other, pre_other, 0, 0)
    own_proj = scatter_sum(grad_proj, y_first)
    own_fc = scatter_sum(grad_fc, x_first)

    grad_heads = dot(grad_attn_full, full_out).astype(BF16)
    grad_outw = dot(grad_attn_full, heads_flat, 0, 0)
    own_outw = scatter_sum(grad_outw, y_first)

    sum_fc = jnp.sum(pre_own.astype(F32), axis=0) + jnp.sum(pre_other.astype(F32), axis=0)
    sums_early = sum_vectors(
        jnp.concatenate(
            [
                grad_gain_two,
                grad_shift_two,
                jnp.sum(grad_attn.astype(F32), axis=0),
                jnp.sum(grad_top, axis=0),
                sum_fc,
            ]
        ),
        4 * width,
    )

    grad_projected = attend_backward(projected, grad_heads, heads_flat, lse)
    grad_own, grad_other = split_rows(grad_projected)
    back_first = swap(dot(grad_other, full_qkv, 1, 1).astype(BF16))
    grad_qkv = dot(normed_first, grad_projected, 0, 0)
    part = (3 * head_width // (2 * PAIR)) * PAIR
    own_qkv = jnp.concatenate(
        [scatter_sum(grad_qkv[:, part:], x_first), scatter_sum(grad_qkv[:, :part], y_first)][::-1],
        axis=1,
    )
    own_qkv = (
        own_qkv.reshape(shard_rows, pairs, 3, PAIR)
        .swapaxes(1, 2)
        .reshape(shard_rows, 3, head_width)
    )
    column_sums = jnp.sum(grad_projected.astype(F32), axis=0).reshape(pairs, 3, PAIR)
    sum_qv = jnp.concatenate(
        [column_sums[:, 0].reshape(head_width), column_sums[:, 2].reshape(head_width)]
    )
    back_first = dot(grad_own, full_qkv, 1, 1) + back_first.astype(F32)
    first_part, grad_gain_one, grad_shift_one = first_back(back_first)
    grad_hidden = (grad_middle + first_part).astype(BF16)
    sums_late = sum_vectors(
        jnp.concatenate([grad_gain_one, grad_shift_one, sum_qv]), 2 * width
    )
    vectors = sums_early[: 4 * width].reshape(4, width)
    return (
        block_out,
        grad_hidden,
        sums_late[:width],
        sums_late[width : 2 * width],
        own_qkv,
        sums_late[2 * width :].reshape(2, head_width),
        own_outw,
        vectors[2],
        vectors[0],
        vectors[1],
        own_fc,
        sums_early[4 * width :],
        own_proj,
        vectors[3],
    )


def solution(mesh):
    placed = (
        P(("dp", "tensor"), None),
        P(),
        P(),
        P("dp", None, "tensor"),
        P(None, "tensor"),
        P("dp", "tensor"),
        P(),
        P(),
        P(),
        P("dp", "tensor"),
        P("tensor"),
        P("dp", "tensor"),
        P(),
        P(("dp", "tensor"), None),
    )
    return jax.shard_map(
        per_device,
        mesh=mesh,
        in_specs=placed,
        out_specs=(
            P(("dp", "tensor"), None),
            P(("dp", "tensor"), None),
            P(),
            P(),
            P("dp", None, "tensor"),
            P(None, "tensor"),
            P("dp", "tensor"),
            P(),
            P(),
            P(),
            P("dp", "tensor"),
            P("tensor"),
            P("dp", "tensor"),
            P(),
        ),
        check_vma=False,
    )
```

```python
import functools
import math

import jax
import jax.numpy as jnp
from jax import lax
from jax.experimental import pallas as pl
from jax.experimental.pallas import tpu as pltpu
from jax.sharding import PartitionSpec as P

HEAD_DIM = 64
SEQ_LEN = 2048
PAIR = 2 * HEAD_DIM
F32 = jnp.float32
BF16 = jnp.bfloat16
VMEM_BYTES = 56 * 1024 * 1024
MASKED = -1e30
SMALL_COST = pl.CostEstimate(flops=1, bytes_accessed=1, transcendentals=0)


def norm_layer(rows_in, gain_vec, shift_vec):
    row_mean = jnp.mean(rows_in, axis=-1, keepdims=True)
    centred = rows_in - row_mean
    variance = jnp.mean(centred * centred, axis=-1, keepdims=True)
    return centred * lax.rsqrt(variance + 1e-05) * gain_vec + shift_vec


def dot(left, right, left_axis=1, right_axis=0):
    return lax.dot_general(
        left, right, (((left_axis,), (right_axis,)), ((), ())), preferred_element_type=F32
    )


def bits_of(count):
    return count.bit_length() - 1


def gather_orders(count):
    even = list(range(bits_of(count)))[::-1]
    odd = even[:-2] + [0, 1]
    if len(even) == 4:
        odd = [2, 3, 0, 1]
    return even, odd


def scatter_orders(count):
    bits = list(range(bits_of(count)))
    return bits, [1, 0] + bits[2:]


def place_info():
    return jnp.stack([lax.axis_index("dp"), lax.axis_index("tensor")]).astype(jnp.int32)


def gathered_owner(info, place, count):
    even, odd = (
        sum(((place >> step) & 1) << bit for step, bit in enumerate(order))
        for order in gather_orders(count)
    )
    return jnp.where(info[1] % 2 == 0, even, odd) ^ info[0]


def scatter_block(info, step, block, sent, count):
    found = []
    for order in scatter_orders(count):
        bit = order[step]
        at = sorted(order[step:]).index(bit)
        own = ((info[0] >> bit) & 1) ^ (1 if sent else 0)
        found.append(((block >> at) << (at + 1)) | (own << at) | (block & ((1 << at) - 1)))
    return jnp.where(info[1] % 2 == 0, found[0], found[1])


def forward_kernel(weight_ref, bias_ref, *refs, rows, halves):
    if halves:
        info_ref, own_ref, other_ref = refs[:3]
        normed_ref, qkv_ref, out_ref, lse_ref, token_ref = refs[-5:]
        half = own_ref.shape[0]
        normed_ref[pl.ds(pl.multiple_of(info_ref[1] * half, half), half), :] = own_ref[...]
        normed_ref[pl.ds(pl.multiple_of((1 - info_ref[1]) * half, half), half), :] = other_ref[...]
    else:
        normed_ref = refs[0]
        qkv_ref, out_ref, lse_ref, token_ref = refs[-4:]
    token_ref[...] = jnp.zeros_like(token_ref)
    qkv_ref[...] = (dot(normed_ref[...], weight_ref[...]) + bias_ref[...]).astype(BF16)
    lane = lax.broadcasted_iota(jnp.int32, (1, PAIR), 1)
    mine = [lane < HEAD_DIM, lane >= HEAD_DIM]
    causal = lax.broadcasted_iota(jnp.int32, (rows, rows), 1) <= lax.broadcasted_iota(
        jnp.int32, (rows, rows), 0
    )
    zero = jnp.zeros((), BF16)
    one = jnp.ones((), BF16)
    scale = jnp.asarray(1.0 / math.sqrt(HEAD_DIM), BF16)
    keys = qkv_ref[:, PAIR : 2 * PAIR]
    values = qkv_ref[:, 2 * PAIR :]
    values_one = [jnp.where(lanes, values, one) for lanes in mine]
    for block in range(SEQ_LEN // rows):
        start = block * rows
        here = pl.ds(start, rows)
        queries = qkv_ref[here, :PAIR] * scale
        halves = []
        for head in range(2):
            query = jnp.where(mine[head], queries, zero)
            near = jnp.where(causal, dot(query, keys[start : start + rows], 1, 1), MASKED)
            top = jnp.max(near, axis=1, keepdims=True)
            if block:
                far = dot(query, keys[:start], 1, 1)
                top = jnp.maximum(top, jnp.max(far, axis=1, keepdims=True))
                far = jnp.exp(far - top).astype(BF16)
            near = jnp.exp(near - top).astype(BF16)
            weighted = dot(near, values_one[head][start : start + rows])
            if block:
                weighted = weighted + dot(far, values_one[head][:start])
            total = pltpu.roll(weighted, HEAD_DIM, 1)
            halves.append(weighted / total)
            lse = top + jnp.log(jnp.where(mine[head], total, weighted))
            lse_ref[head : head + 1, here] = jnp.transpose(lse)[0:1]
        out_ref[here, :] = jnp.where(mine[0], halves[0], halves[1]).astype(BF16)


def to_row(columns):
    folded = sum(columns[:, c : c + 128] for c in range(0, columns.shape[1], 128))
    return jnp.sum(jnp.transpose(folded), axis=0, keepdims=True)


def backward_kernel(
    info_ref,
    qkv_ref,
    heads_ref,
    lse_ref,
    own_ref,
    other_ref,
    normed_ref,
    weight_ref,
    out_weight_ref,
    norm_ref,
    *refs,
    rows,
    ties,
    kind,
):
    before_ref = refs[0]
    result_ref, sums_ref, vector_ref, token_ref = refs[ties : ties + 4]
    grad_ref, dq_ref, product_ref = refs[-3:]
    token_ref[...] = jnp.zeros_like(token_ref)
    tokens = qkv_ref.shape[0]
    part = own_ref.shape[0]
    grad_ref[pl.ds(pl.multiple_of(info_ref[1] * part, part), part), :] = own_ref[...]
    grad_ref[pl.ds(pl.multiple_of((1 - info_ref[1]) * part, part), part), :] = other_ref[...]

    lane = lax.broadcasted_iota(jnp.int32, (1, PAIR), 1)
    mine = [lane < HEAD_DIM, lane >= HEAD_DIM]
    causal = lax.broadcasted_iota(jnp.int32, (rows, rows), 0) <= lax.broadcasted_iota(
        jnp.int32, (rows, rows), 1
    )
    zero = jnp.zeros((), BF16)
    scale = jnp.asarray(1.0 / math.sqrt(HEAD_DIM), BF16)
    grad = dot(grad_ref[...], out_weight_ref[...]).astype(BF16)
    out = heads_ref[...]
    queries = [jnp.where(lanes, qkv_ref[:, :PAIR], zero) * scale for lanes in mine]
    grads = [jnp.where(lanes, grad, zero) for lanes in mine]
    product = jnp.transpose(grad.astype(F32) * out.astype(F32))
    delta = [
        jnp.sum(product[:HEAD_DIM], axis=0, keepdims=True),
        jnp.sum(product[HEAD_DIM:], axis=0, keepdims=True),
    ]
    for block in range(tokens // rows):
        start = block * rows
        here = pl.ds(start, rows)
        keys = qkv_ref[here, PAIR : 2 * PAIR]
        values = qkv_ref[here, 2 * PAIR :]
        keys_turned = jnp.transpose(keys * scale)
        key_grad = jnp.zeros((rows, PAIR), F32)
        value_grad = jnp.zeros((rows, PAIR), F32)
        for head in range(2):
            part = slice(HEAD_DIM * head, HEAD_DIM * (head + 1))
            for low, high in ((start, start + rows), (start + rows, tokens)):
                if low == high:
                    continue
                scores = dot(keys, queries[head][low:high], 1, 1)
                if low == start:
                    scores = jnp.where(causal, scores, MASKED)
                probs = jnp.exp(scores - lse_ref[head : head + 1, low:high])
                grad_probs = dot(values, grads[head][low:high], 1, 1)
                grad_scores = (probs * (grad_probs - delta[head][:, low:high])).astype(BF16)
                value_grad = value_grad + dot(probs.astype(BF16), grads[head][low:high])
                key_grad = key_grad + dot(grad_scores, queries[head][low:high])
                turned = dot(keys_turned[part], grad_scores)
                if block == 0:
                    dq_ref[part, low:high] = turned
                else:
                    dq_ref[part, low:high] += turned
        result_ref[here, PAIR : 2 * PAIR] = key_grad.astype(BF16)
        result_ref[here, 2 * PAIR :] = value_grad.astype(BF16)
    result_ref[:, :PAIR] = jnp.transpose(dq_ref[...]).astype(BF16)

    result = result_ref[...]
    sums = jnp.sum(result.astype(F32), axis=0, keepdims=True)
    sums_ref[...] = sums
    weight_grad = jnp.transpose(dot(result, normed_ref[...], 0, 0))
    out_weight_grad = jnp.transpose(dot(out, grad_ref[...], 0, 0))
    high = sums.astype(BF16)
    low = (sums - high.astype(F32)).astype(BF16)
    weight = weight_ref[...]
    shift = dot(high, weight, 1, 1) + dot(low, weight, 1, 1)
    gain = (to_row(weight.astype(F32) * weight_grad) - norm_ref[1:2, :] * shift) / norm_ref[0:1, :]
    vector_ref[0:1, :] = gain
    vector_ref[1:2, :] = shift
    wide = weight_grad.shape[1]
    if kind == "flat":
        whole_ref = refs[ties + 4]
        whole_ref[:, :wide] = weight_grad
        whole_ref[:, wide:] = out_weight_grad
        return
    target = refs[ties + 4] if kind == "whole" else product_ref
    count, shard = target.shape[:2]
    target[:, :, :wide] = weight_grad.reshape(count, shard, wide)
    target[:, :, wide:] = out_weight_grad.reshape(count, shard, PAIR)
    if kind == "whole":
        return
    kept_ref, away_ref = refs[ties + 4 : ties + 6]
    for block in range(count // 2):
        keep = scatter_block(info_ref, 0, block, False, count)
        send = scatter_block(info_ref, 0, block, True, count)
        start = 0
        if kind == "joined":
            start = before_ref.shape[2]
            kept_ref[block, :, :start] = before_ref[keep]
            away_ref[block, :, :start] = before_ref[send].astype(BF16)
        kept_ref[block, :, start:] = product_ref[keep]
        away_ref[block, :, start:] = product_ref[send].astype(BF16)


def feed_forward_kernel(
    info_ref,
    own_ref,
    other_ref,
    cot_own_ref,
    cot_other_ref,
    bias_ref,
    *refs,
    blocks,
    placed,
):
    weights, refs = refs[: 2 if placed else 4], refs[2 if placed else 4 :]
    terms_own_ref, terms_other_ref, back_own_ref, back_other_ref, sums_ref = refs[:5]
    refs = refs[5:]
    step = pl.program_id(0)
    own = step < blocks
    if placed:
        grad_fc_ref, grad_proj_ref = refs
        fc, proj = (ref[...] for ref in weights)
    else:
        kept_ref, away_ref, fc_ref, proj_ref, grad_fc_ref, grad_proj_ref, away_scratch, sems = refs
        count = fc_ref.shape[0]
        half = count // 2

        @pl.when(step == 0)
        def _():
            copies = []
            for number, target in enumerate((fc_ref, proj_ref)):
                for place in range(count):
                    source = weights[2 * number + place // half].at[place % half]
                    copies.append(
                        pltpu.make_async_copy(
                            source,
                            target.at[gathered_owner(info_ref, place, count)],
                            sems.at[number * count + place],
                        )
                    )
                    copies[-1].start()
            for copy in copies:
                copy.wait()

        fc, proj = (ref[...].reshape(-1, ref.shape[2]) for ref in (fc_ref, proj_ref))

    @pl.when(step == 0)
    def _():
        sums_ref[...] = jnp.zeros_like(sums_ref)
        grad_fc_ref[...] = jnp.zeros_like(grad_fc_ref)
        grad_proj_ref[...] = jnp.zeros_like(grad_proj_ref)

    rows = jnp.where(own, own_ref[...], other_ref[...])
    cot = jnp.where(own, cot_own_ref[...], cot_other_ref[...])
    pre = dot(rows, fc) + bias_ref[...]
    slope = math.sqrt(2.0 / math.pi)
    square = pre * pre
    bent = jnp.tanh(slope * pre * (1.0 + 0.044715 * square))
    upper = 0.5 * (1.0 + bent)
    act = (pre * upper).astype(BF16)
    terms = dot(act, proj, 1, 1)
    grad_proj_ref[...] += dot(cot, act, 0, 0).reshape(grad_proj_ref.shape)
    derivative = upper + 0.5 * pre * (1.0 - bent * bent) * (
        slope * (1.0 + 3.0 * 0.044715 * square)
    )
    grad_pre = (dot(cot, proj) * derivative).astype(BF16)
    back = dot(grad_pre, fc, 1, 1)
    grad_fc_ref[...] += dot(rows, grad_pre, 0, 0).reshape(grad_fc_ref.shape)
    sums_ref[...] += jnp.sum(grad_pre.astype(F32), axis=0, keepdims=True)

    @pl.when(own)
    def _():
        terms_own_ref[...] = terms
        back_own_ref[...] = back

    @pl.when(jnp.logical_not(own))
    def _():
        terms_other_ref[...] = terms.astype(BF16)
        back_other_ref[...] = back.astype(BF16)

    if not placed:
        hidden = fc_ref.shape[2]

        @pl.when(step == 2 * blocks - 1)
        def _():
            copies = []
            for number, grad_ref in enumerate((grad_fc_ref, grad_proj_ref)):
                for block in range(half):
                    copies.append(
                        pltpu.make_async_copy(
                            grad_ref.at[scatter_block(info_ref, 0, block, False, count)],
                            kept_ref.at[block, :, pl.ds(number * hidden, hidden)],
                            sems.at[number * half + block],
                        )
                    )
                    copies[-1].start()
            for number, grad_ref in enumerate((grad_fc_ref, grad_proj_ref)):
                for block in range(half):
                    away_scratch[block, :, number * hidden : (number + 1) * hidden] = grad_ref[
                        scatter_block(info_ref, 0, block, True, count)
                    ].astype(BF16)
            send = pltpu.make_async_copy(away_scratch, away_ref, sems.at[2 * half])
            send.start()
            for copy in copies + [send]:
                copy.wait()


ANY_SPEC = pl.BlockSpec(memory_space=pl.ANY)
TOKEN_SHAPE = jax.ShapeDtypeStruct((1, 1), F32)
TOKEN_SPEC = pl.BlockSpec((1, 1), lambda *_: (0, 0))


def attend_forward(pair, normed, weight, bias, ties):
    halves = isinstance(normed, tuple)
    tokens = 2 * normed[1].shape[0] if halves else normed.shape[0]
    features, columns = weight.shape
    every = pl.BlockSpec((tokens, features), lambda: (0, 0))
    in_specs = [
        pl.BlockSpec((features, columns), lambda: (0, 0)),
        pl.BlockSpec((1, columns), lambda: (0, 0)),
    ]
    out_specs = [
        pl.BlockSpec((tokens, columns), lambda: (0, 0)),
        pl.BlockSpec((tokens, PAIR), lambda: (0, 0)),
        pl.BlockSpec((2, tokens), lambda: (0, 0)),
        pl.BlockSpec((1, 1), lambda: (0, 0)),
    ]
    out_shape = [
        jax.ShapeDtypeStruct((tokens, columns), BF16),
        jax.ShapeDtypeStruct((tokens, PAIR), BF16),
        jax.ShapeDtypeStruct((2, tokens), F32),
        TOKEN_SHAPE,
    ]
    if halves:
        half = pl.BlockSpec((tokens // 2, features), lambda: (0, 0))
        in_specs += [pl.BlockSpec(memory_space=pltpu.SMEM), half, half]
        out_specs = [every] + out_specs
        out_shape = [jax.ShapeDtypeStruct((tokens, features), BF16)] + out_shape
    else:
        in_specs += [every]
    in_specs += [ANY_SPEC] * len(ties)
    out = pl.pallas_call(
        functools.partial(forward_kernel, rows=512, halves=halves),
        in_specs=in_specs,
        out_specs=out_specs,
        out_shape=out_shape,
        compiler_params=pltpu.CompilerParams(vmem_limit_bytes=VMEM_BYTES),
        cost_estimate=SMALL_COST,
        name=f"attend_forward_{pair}",
    )(weight, bias, *(normed if halves else (normed,)), *ties)
    return out[0] if halves else normed, *out[-4:-1], out[-1].reshape(())


def attend_backward(
    pair, kind, projected, heads_flat, lse, info, own, other, normed, weight, out_weight, norm, ties
):
    tokens, columns = projected.shape
    features = normed.shape[1]
    count = lax.axis_size("dp")
    shard = features // count
    fixed = lambda shape: pl.BlockSpec(shape, lambda _: (0,) * len(shape))
    scalars = pl.BlockSpec(memory_space=pltpu.SMEM)
    out_shape = [
        jax.ShapeDtypeStruct((tokens, columns), BF16),
        jax.ShapeDtypeStruct((1, columns), F32),
        jax.ShapeDtypeStruct((2, features), F32),
        TOKEN_SHAPE,
    ]
    wide = 4 * PAIR
    product = pltpu.VMEM((8, 128), F32)
    tie_specs = [ANY_SPEC] * len(ties)
    if shard % 16:
        inner = "flat"
        out_shape += [jax.ShapeDtypeStruct((features, wide), F32)]
    elif kind == "whole":
        inner = kind
        out_shape += [jax.ShapeDtypeStruct((count, shard, wide), F32)]
    else:
        inner = kind
        width = wide
        if kind == "joined":
            width += ties[0].shape[2]
            tie_specs[0] = fixed(ties[0].shape)
        out_shape += [
            jax.ShapeDtypeStruct((count // 2, shard, width), held) for held in (F32, BF16)
        ]
        product = pltpu.VMEM((count, shard, wide), F32)
    out = pl.pallas_call(
        functools.partial(backward_kernel, rows=256, ties=len(ties), kind=inner),
        grid=(1,),
        in_specs=[
            scalars,
            fixed(projected.shape),
            pl.BlockSpec((tokens, PAIR), lambda _: (0, pair)),
            fixed(lse.shape),
            fixed(own.shape),
            fixed(other.shape),
            fixed(normed.shape),
            pl.BlockSpec((features, columns), lambda _: (0, pair)),
            pl.BlockSpec((features, PAIR), lambda _: (0, pair)),
            fixed(norm.shape),
        ]
        + tie_specs,
        out_specs=[fixed(result.shape) for result in out_shape],
        out_shape=out_shape,
        scratch_shapes=[
            pltpu.VMEM((tokens, features), BF16),
            pltpu.VMEM((PAIR, tokens), F32),
            product,
        ],
        compiler_params=pltpu.CompilerParams(vmem_limit_bytes=VMEM_BYTES),
        cost_estimate=SMALL_COST,
        name=f"attend_backward_{pair}",
    )(info, projected, heads_flat, lse, own, other, normed, weight, out_weight, norm, *ties)
    if kind == "whole":
        gradient = out[4]
    elif shard % 16:
        gradient = Scatter(out[4] if kind == "split" else jnp.concatenate([ties[0], out[4]], axis=1))
    else:
        gradient = Scatter(out[4], out[5])
    return out[0], out[1], out[2], out[3], gradient


def feed_forward(info, own, other, cot_own, cot_other, bias, fc, proj):
    tokens, features = own.shape
    hidden = bias.shape[0]
    block = 512
    blocks = tokens // block
    count = lax.axis_size("dp")
    shard = features // count
    placed = shard % 16 != 0
    first = pl.BlockSpec((block, features), lambda i: (jnp.minimum(i, blocks - 1), 0))
    second = pl.BlockSpec((block, features), lambda i: (jnp.maximum(i - blocks, 0), 0))
    out_specs = [first, second, first, second, pl.BlockSpec((1, hidden), lambda i: (0, 0))]
    out_shape = [
        jax.ShapeDtypeStruct((tokens, features), kind) for kind in (F32, BF16, F32, BF16)
    ] + [jax.ShapeDtypeStruct((1, hidden), F32)]
    scratch = []
    weights = [fc.held, fc.got, proj.held, proj.got]
    weight_specs = [ANY_SPEC] * 4
    if placed:
        weights = [fc.result(), proj.result()]
        weight_specs = [pl.BlockSpec((features, hidden), lambda i: (0, 0))] * 2
        out_specs += [pl.BlockSpec((features, hidden), lambda i: (0, 0))] * 2
        out_shape += [jax.ShapeDtypeStruct((features, hidden), F32)] * 2
    else:
        out_specs += [ANY_SPEC] * 2
        out_shape += [
            jax.ShapeDtypeStruct((count // 2, shard, 2 * hidden), kind) for kind in (F32, BF16)
        ]
        scratch = [
            pltpu.VMEM((count, shard, hidden), BF16),
            pltpu.VMEM((count, shard, hidden), BF16),
            pltpu.VMEM((count, shard, hidden), F32),
            pltpu.VMEM((count, shard, hidden), F32),
            pltpu.VMEM((count // 2, shard, 2 * hidden), BF16),
            pltpu.SemaphoreType.DMA((2 * count,)),
        ]
    out = pl.pallas_call(
        functools.partial(feed_forward_kernel, blocks=blocks, placed=placed),
        grid=(2 * blocks,),
        in_specs=[
            pl.BlockSpec(memory_space=pltpu.SMEM),
            first,
            second,
            first,
            second,
            pl.BlockSpec((1, hidden), lambda i: (0, 0)),
        ]
        + weight_specs,
        out_specs=out_specs,
        out_shape=out_shape,
        scratch_shapes=scratch,
        compiler_params=pltpu.CompilerParams(vmem_limit_bytes=VMEM_BYTES),
        cost_estimate=SMALL_COST,
        name="feed_forward",
    )(info, own, other, cot_own, cot_other, bias.reshape(1, hidden), *weights)
    if placed:
        return (*out[:5], Scatter(jnp.concatenate(out[5:], axis=1)))
    return (*out[:5], Scatter(*out[5:]))


def exchange(block, bits):
    count = lax.axis_size("dp")
    width = lax.axis_size("tensor")
    pairs = [
        (i * width + t, (i ^ (1 << bits[t % 2])) * width + t)
        for i in range(count)
        for t in range(width)
    ]
    return lax.ppermute(block, ("dp", "tensor"), pairs)


def swap(block):
    count = lax.axis_size("tensor")
    return lax.ppermute(block, "tensor", [(i, count - 1 - i) for i in range(count)])


class Gather:
    def __init__(self, shard):
        self.orders = list(zip(*gather_orders(lax.axis_size("dp"))))
        self.held = shard[None]
        self.step = 0
        self.got = exchange(self.held, self.orders[0])

    def advance(self, token=None):
        self.step += 1
        if self.step < len(self.orders):
            joined = [self.held, self.got]
            if token is not None:
                joined = [part + token.astype(BF16) for part in joined]
            self.held = jnp.concatenate(joined, axis=0)
            self.got = exchange(self.held, self.orders[self.step])
        return self

    def result(self, token=None):
        while self.step < len(self.orders) - 1:
            self.advance()
        return place_rows(place_info(), self.held, self.got, token)


def place_kernel(info_ref, token_ref, held_ref, got_ref, out_ref, sems):
    half = held_ref.shape[0]
    copies = []
    for place in range(2 * half):
        source = held_ref.at[place] if place < half else got_ref.at[place - half]
        owner = gathered_owner(info_ref, place, 2 * half)
        copies.append(pltpu.make_async_copy(source, out_ref.at[owner], sems.at[place]))
        copies[-1].start()
    for copy in copies:
        copy.wait()


def place_rows(info, held, got, token=None):
    half, rows, columns = held.shape
    count = 2 * half
    if rows % 16:
        owners = gathered_owner(info, jnp.arange(count, dtype=jnp.int32), count)
        placed = jnp.concatenate([held, got], axis=0)[jnp.argsort(owners)]
        return placed.reshape(count * rows, columns)
    placed = pl.pallas_call(
        place_kernel,
        in_specs=[pl.BlockSpec(memory_space=pltpu.SMEM)] * 2 + [ANY_SPEC] * 2,
        out_specs=pl.BlockSpec(memory_space=pltpu.VMEM),
        out_shape=jax.ShapeDtypeStruct((count, rows, columns), BF16),
        scratch_shapes=[pltpu.SemaphoreType.DMA((count,))],
        compiler_params=pltpu.CompilerParams(vmem_limit_bytes=16 * 1024 * 1024),
        cost_estimate=SMALL_COST,
        name="place_rows",
    )(info, jnp.zeros((1, 1), F32) if token is None else token.reshape(1, 1), held, got)
    return placed.reshape(count * rows, columns)


def join_kernel(info_ref, token_ref, keep_ref, send_ref, got_keep_ref, got_send_ref, *refs):
    kept_ref, away_ref = refs[-2:]
    kept_ref[...] = keep_ref[...] + got_keep_ref[...].astype(F32)
    away_ref[...] = (send_ref[...] + got_send_ref[...].astype(F32)).astype(BF16)


def join_halves(info, step, held, got, token, ties):
    count, rows, columns = held.shape
    half = count // 2
    size = lax.axis_size("dp")

    def at(sent):
        return pl.BlockSpec(
            (1, rows, columns), lambda i, info: (scatter_block(info, step, i, sent, size), 0, 0)
        )

    result = pl.BlockSpec((1, rows, columns), lambda i, info: (i, 0, 0))
    return pl.pallas_call(
        join_kernel,
        grid_spec=pltpu.PrefetchScalarGridSpec(
            num_scalar_prefetch=1,
            grid=(half,),
            in_specs=[pl.BlockSpec(memory_space=pltpu.SMEM), at(False), at(True), at(False), at(True)]
            + [ANY_SPEC] * len(ties),
            out_specs=[result, result],
        ),
        out_shape=[jax.ShapeDtypeStruct((half, rows, columns), kind) for kind in (F32, BF16)],
        compiler_params=pltpu.CompilerParams(vmem_limit_bytes=16 * 1024 * 1024),
        cost_estimate=SMALL_COST,
        name="join_halves",
    )(info, jnp.zeros((1, 1), F32) if token is None else token, held, held, got, got, *ties)


class Scatter:
    def __init__(self, whole, away=None):
        self.orders = list(zip(*scatter_orders(lax.axis_size("dp"))))
        self.step = 0
        if away is None:
            count = lax.axis_size("dp")
            self.split(whole.reshape(count, whole.shape[0] // count, whole.shape[1]))
        else:
            self.kept, self.away = whole, away
        self.got = exchange(self.away, self.orders[0])

    def split(self, held):
        count = lax.axis_size("dp")
        blocks = jnp.arange(held.shape[0] // 2, dtype=jnp.int32)
        keep, send = (
            scatter_block(place_info(), self.step, blocks, sent, count) for sent in (False, True)
        )
        self.kept = jnp.take(held, keep, axis=0)
        self.away = jnp.take(held, send, axis=0).astype(BF16)

    def advance(self, token=None, ties=()):
        self.step += 1
        if self.kept.shape[1] % 16:
            self.split(self.kept + self.got.astype(F32))
        else:
            self.kept, self.away = join_halves(
                place_info(), self.step, self.kept, self.got, token, ties
            )
        self.got = exchange(self.away, self.orders[self.step])

    def result(self):
        while self.step < len(self.orders) - 1:
            self.advance()
        return (self.kept + self.got.astype(F32))[0]


def sum_vectors(vector, both):
    for bit in range(bits_of(lax.axis_size("dp"))):
        vector = vector + exchange(vector, (bit, bit))
    return jnp.concatenate([vector[:both] + swap(vector[:both]), vector[both:]])


def per_device(
    hidden_in,
    first_gain,
    first_shift,
    qkv_weight,
    qv_bias,
    out_weight,
    out_bias,
    second_gain,
    second_shift,
    fc_weight,
    fc_bias,
    proj_weight,
    proj_bias,
    cotangent,
):
    tensor_pos = lax.axis_index("tensor")
    half = hidden_in.shape[0]
    width = hidden_in.shape[1]
    shard_rows = qkv_weight.shape[0]
    head_width = qkv_weight.shape[2]
    pairs = head_width // PAIR
    columns = 3 * PAIR

    def split_rows(whole):
        own = lax.dynamic_slice_in_dim(whole, tensor_pos * half, half, 0)
        other = lax.dynamic_slice_in_dim(whole, (1 - tensor_pos) * half, half, 0)
        return own, other

    by_pair = qkv_weight.reshape(shard_rows, 3, pairs, PAIR).swapaxes(1, 2)
    by_pair = by_pair.reshape(shard_rows, pairs * columns)
    first_gather = Gather(by_pair[:, :columns])
    rest_gather = Gather(jnp.concatenate([by_pair[:, columns:], out_weight], axis=1))
    fc_gather = Gather(fc_weight)
    proj_gather = Gather(proj_weight)

    rows_first = hidden_in.astype(F32)
    row_mean = jnp.mean(rows_first, axis=-1, keepdims=True)
    centred = rows_first - row_mean
    first_rsqrt = lax.rsqrt(jnp.mean(centred * centred, axis=-1, keepdims=True) + 1e-05)
    normed_piece = (centred * first_rsqrt * first_gain + first_shift).astype(BF16)
    info = place_info()
    normed_first = (info, normed_piece, swap(normed_piece))
    cot_other = swap(cotangent)

    bias_parts = jnp.stack([qv_bias[0], jnp.zeros_like(qv_bias[0]), qv_bias[1]])
    bias_cols = bias_parts.reshape(3, pairs, PAIR).swapaxes(0, 1).reshape(pairs, 1, columns)
    fc_gather.advance()
    proj_gather.advance()
    full_qkv = [first_gather.result()]
    projected, heads, lses = [], [], []
    for pair in range(pairs):
        weight = full_qkv[pair]
        normed_first, columns_out, heads_out, lse, token = attend_forward(
            pair,
            normed_first,
            weight,
            bias_cols[pair],
            [fc_gather.held, proj_gather.held] if pair else [],
        )
        projected.append(columns_out)
        heads.append(heads_out)
        lses.append(lse)
        if pair == 0:
            rest = rest_gather.result(token)
            full_qkv += [
                rest[:, p * columns : (p + 1) * columns] for p in range(pairs - 1)
            ]
            full_out = rest[:, (pairs - 1) * columns :]
        if pair < pairs - 1:
            fc_gather.advance(token)
            proj_gather.advance(token)
    full_qkv = jnp.concatenate(full_qkv, axis=1)
    heads_flat = jnp.concatenate(heads, axis=1)
    heads_own, heads_other = split_rows(heads_flat)
    attn_other = swap(dot(heads_other, full_out, 1, 1).astype(BF16))
    middle = rows_first + (dot(heads_own, full_out, 1, 1) + attn_other.astype(F32)) + out_bias

    normed_mid, second_back = jax.vjp(norm_layer, middle, second_gain, second_shift)
    normed_own = normed_mid.astype(BF16)
    normed_other = swap(normed_own)

    terms_own, terms_other, back_own, back_other, sum_fc, ff_sum = feed_forward(
        info, normed_own, normed_other, cotangent, cot_other, fc_bias, fc_gather, proj_gather
    )
    back_other = swap(back_other)
    terms_other = swap(terms_other)
    block_out = (middle + (terms_own + terms_other.astype(F32)) + proj_bias).astype(BF16)
    back_second = back_own + back_other.astype(F32)

    grad_top = cotangent.astype(F32)
    mid_part, grad_gain_two, grad_shift_two = second_back(back_second)
    grad_middle = grad_top + mid_part
    grad_attn = grad_middle.astype(BF16)
    grad_attn_other = swap(grad_attn)
    hidden = fc_weight.shape[1]
    early = jnp.concatenate(
        [
            grad_gain_two,
            grad_shift_two,
            jnp.sum(grad_attn.astype(F32), axis=0),
            jnp.sum(grad_top, axis=0),
            sum_fc.reshape(-1),
        ]
    )

    norm_first = jnp.stack([first_gain, first_shift])
    shared = (info, grad_attn, grad_attn_other, normed_first, full_qkv, full_out, norm_first)
    kinds = ["split"] + ["whole"] * (pairs - 2) + ["joined"]
    results, column_sums, vector_parts = [], [], []
    first_sum = rest_sum = whole = None
    for pair in range(pairs):
        ties = [] if whole is None else [whole]
        if pair:
            ties += [ff_sum.away, first_sum.away]
        result, sums, vector, token, gradient = attend_backward(
            pair, kinds[pair], projected[pair], heads_flat, lses[pair], *shared, ties
        )
        results.append(result)
        column_sums.append(sums)
        vector_parts.append(vector)
        ff_sum.advance(token)
        if pair:
            first_sum.advance(token)
        if pair == 0:
            first_sum = gradient
        elif pair == pairs - 1:
            rest_sum = gradient
        else:
            whole = gradient
    grad_projected = jnp.concatenate(results, axis=1)
    grad_own, grad_other = split_rows(grad_projected)
    back_other = dot(grad_other, full_qkv, 1, 1).astype(BF16)
    back_own = dot(grad_own, full_qkv, 1, 1)
    back_first = back_own + swap(back_other).astype(F32)
    rest_sum.advance(ties=(back_other,))
    vector_parts = sum(vector_parts[1:], vector_parts[0])
    column_sums = jnp.concatenate(column_sums, axis=0).reshape(pairs, 3, PAIR)
    vectors = sum_vectors(
        jnp.concatenate(
            [
                vector_parts.reshape(-1),
                early,
                column_sums[:, 0].reshape(-1),
                column_sums[:, 2].reshape(-1),
            ]
        ),
        6 * width,
    )
    scaled = back_first * first_gain
    normalised = centred * first_rsqrt
    grad_hidden = grad_middle + first_rsqrt * (
        scaled
        - jnp.mean(scaled, axis=-1, keepdims=True)
        - normalised * jnp.mean(scaled * normalised, axis=-1, keepdims=True)
    )
    own_heads = jnp.concatenate([first_sum.result(), rest_sum.result()], axis=1).reshape(
        shard_rows, pairs, 4, PAIR
    )
    own_outw = own_heads[:, :, 3].reshape(shard_rows, head_width)
    own_qkv = own_heads[:, :, :3].swapaxes(1, 2).reshape(shard_rows, 3, head_width)
    own_ff = ff_sum.result()
    sums = vectors[: 6 * width].reshape(6, width)
    hidden_sums = vectors[6 * width : 6 * width + hidden]
    return (
        block_out,
        grad_hidden.astype(BF16),
        sums[0],
        sums[1],
        own_qkv,
        vectors[6 * width + hidden :].reshape(2, head_width),
        own_outw,
        sums[4],
        sums[2],
        sums[3],
        own_ff[:, :hidden],
        hidden_sums,
        own_ff[:, hidden:],
        sums[5],
    )


def solution(mesh):
    placed = (
        P(("dp", "tensor"), None),
        P(),
        P(),
        P("dp", None, "tensor"),
        P(None, "tensor"),
        P("dp", "tensor"),
        P(),
        P(),
        P(),
        P("dp", "tensor"),
        P("tensor"),
        P("dp", "tensor"),
        P(),
        P(("dp", "tensor"), None),
    )
    return jax.shard_map(
        per_device,
        mesh=mesh,
        in_specs=placed,
        out_specs=(
            P(("dp", "tensor"), None),
            P(("dp", "tensor"), None),
            P(),
            P(),
            P("dp", None, "tensor"),
            P(None, "tensor"),
            P("dp", "tensor"),
            P(),
            P(),
            P(),
            P("dp", "tensor"),
            P("tensor"),
            P("dp", "tensor"),
            P(),
        ),
        check_vma=False,
    )
```

```python
import functools
import math

import jax
import jax.numpy as jnp
from jax import lax
from jax.experimental import pallas as pl
from jax.experimental.pallas import tpu as pltpu
from jax.sharding import PartitionSpec as P

HEAD_DIM = 64
SEQ_LEN = 2048
PAIR = 2 * HEAD_DIM
F32 = jnp.float32
BF16 = jnp.bfloat16
VMEM_BYTES = 56 * 1024 * 1024
MASKED = -1e30
SMALL_COST = pl.CostEstimate(flops=1, bytes_accessed=1, transcendentals=0)


def norm_layer(rows_in, gain_vec, shift_vec):
    row_mean = jnp.mean(rows_in, axis=-1, keepdims=True)
    centred = rows_in - row_mean
    variance = jnp.mean(centred * centred, axis=-1, keepdims=True)
    return centred * lax.rsqrt(variance + 1e-05) * gain_vec + shift_vec


def dot(left, right, left_axis=1, right_axis=0):
    return lax.dot_general(
        left, right, (((left_axis,), (right_axis,)), ((), ())), preferred_element_type=F32
    )


def bits_of(count):
    return count.bit_length() - 1


def gather_orders(count):
    even = list(range(bits_of(count)))[::-1]
    odd = even[:-2] + [0, 1]
    if len(even) == 4:
        odd = [2, 3, 0, 1]
    return even, odd


def scatter_orders(count):
    bits = list(range(bits_of(count)))
    return bits, [1, 0] + bits[2:]


def place_info():
    return jnp.stack([lax.axis_index("dp"), lax.axis_index("tensor")]).astype(jnp.int32)


def gathered_owner(info, place, count):
    even, odd = (
        sum(((place >> step) & 1) << bit for step, bit in enumerate(order))
        for order in gather_orders(count)
    )
    return jnp.where(info[1] % 2 == 0, even, odd) ^ info[0]


def scatter_block(info, step, block, sent, count):
    found = []
    for order in scatter_orders(count):
        bit = order[step]
        at = sorted(order[step:]).index(bit)
        own = ((info[0] >> bit) & 1) ^ (1 if sent else 0)
        found.append(((block >> at) << (at + 1)) | (own << at) | (block & ((1 << at) - 1)))
    return jnp.where(info[1] % 2 == 0, found[0], found[1])


def forward_kernel(weight_ref, bias_ref, *refs, rows, halves):
    if halves:
        info_ref, own_ref, other_ref = refs[:3]
        normed_ref, qkv_ref, out_ref, lse_ref, token_ref = refs[-5:]
        half = own_ref.shape[0]
        normed_ref[pl.ds(pl.multiple_of(info_ref[1] * half, half), half), :] = own_ref[...]
        normed_ref[pl.ds(pl.multiple_of((1 - info_ref[1]) * half, half), half), :] = other_ref[...]
    else:
        normed_ref = refs[0]
        qkv_ref, out_ref, lse_ref, token_ref = refs[-4:]
    token_ref[...] = jnp.zeros_like(token_ref)
    qkv_ref[...] = (dot(normed_ref[...], weight_ref[...]) + bias_ref[...]).astype(BF16)
    lane = lax.broadcasted_iota(jnp.int32, (1, PAIR), 1)
    mine = [lane < HEAD_DIM, lane >= HEAD_DIM]
    causal = lax.broadcasted_iota(jnp.int32, (rows, rows), 1) <= lax.broadcasted_iota(
        jnp.int32, (rows, rows), 0
    )
    zero = jnp.zeros((), BF16)
    one = jnp.ones((), BF16)
    scale = jnp.asarray(1.0 / math.sqrt(HEAD_DIM), BF16)
    keys = qkv_ref[:, PAIR : 2 * PAIR]
    values = qkv_ref[:, 2 * PAIR :]
    values_one = [jnp.where(lanes, values, one) for lanes in mine]
    for block in range(SEQ_LEN // rows):
        start = block * rows
        here = pl.ds(start, rows)
        queries = qkv_ref[here, :PAIR] * scale
        halves = []
        for head in range(2):
            query = jnp.where(mine[head], queries, zero)
            near = jnp.where(causal, dot(query, keys[start : start + rows], 1, 1), MASKED)
            top = jnp.max(near, axis=1, keepdims=True)
            if block:
                far = dot(query, keys[:start], 1, 1)
                top = jnp.maximum(top, jnp.max(far, axis=1, keepdims=True))
                far = jnp.exp(far - top).astype(BF16)
            near = jnp.exp(near - top).astype(BF16)
            weighted = dot(near, values_one[head][start : start + rows])
            if block:
                weighted = weighted + dot(far, values_one[head][:start])
            total = pltpu.roll(weighted, HEAD_DIM, 1)
            halves.append(weighted / total)
            lse = top + jnp.log(jnp.where(mine[head], total, weighted))
            lse_ref[head : head + 1, here] = jnp.transpose(lse)[0:1]
        out_ref[here, :] = jnp.where(mine[0], halves[0], halves[1]).astype(BF16)


def to_row(columns):
    folded = sum(columns[:, c : c + 128] for c in range(0, columns.shape[1], 128))
    return jnp.sum(jnp.transpose(folded), axis=0, keepdims=True)


def backward_kernel(
    info_ref,
    qkv_ref,
    heads_ref,
    lse_ref,
    own_ref,
    other_ref,
    normed_ref,
    weight_ref,
    out_weight_ref,
    norm_ref,
    *refs,
    rows,
    ties,
    kind,
):
    before_ref = refs[0]
    result_ref, sums_ref, vector_ref, token_ref = refs[ties : ties + 4]
    grad_ref, dq_ref, product_ref, rows_ref, sems = refs[-5:]
    token_ref[...] = jnp.zeros_like(token_ref)
    tokens = qkv_ref.shape[0]
    part = own_ref.shape[0]
    own_rows = pl.ds(pl.multiple_of(info_ref[1] * part, part), part)
    other_rows = pl.ds(pl.multiple_of((1 - info_ref[1]) * part, part), part)
    own_copy = pltpu.make_async_copy(own_ref, grad_ref.at[own_rows, :], sems.at[0])
    other_copy = pltpu.make_async_copy(other_ref, grad_ref.at[other_rows, :], sems.at[1])
    rows_copy = pltpu.make_async_copy(normed_ref, rows_ref, sems.at[2])
    own_copy.start()
    other_copy.start()
    rows_copy.start()
    own_copy.wait()
    other_copy.wait()

    lane = lax.broadcasted_iota(jnp.int32, (1, PAIR), 1)
    mine = [lane < HEAD_DIM, lane >= HEAD_DIM]
    causal = lax.broadcasted_iota(jnp.int32, (rows, rows), 0) <= lax.broadcasted_iota(
        jnp.int32, (rows, rows), 1
    )
    zero = jnp.zeros((), BF16)
    scale = jnp.asarray(1.0 / math.sqrt(HEAD_DIM), BF16)
    grad = dot(grad_ref[...], out_weight_ref[...]).astype(BF16)
    out = heads_ref[...]
    queries = [jnp.where(lanes, qkv_ref[:, :PAIR], zero) * scale for lanes in mine]
    grads = [jnp.where(lanes, grad, zero) for lanes in mine]
    product = jnp.transpose(grad.astype(F32) * out.astype(F32))
    delta = [
        jnp.sum(product[:HEAD_DIM], axis=0, keepdims=True),
        jnp.sum(product[HEAD_DIM:], axis=0, keepdims=True),
    ]
    for block in range(tokens // rows):
        start = block * rows
        here = pl.ds(start, rows)
        keys = qkv_ref[here, PAIR : 2 * PAIR]
        values = qkv_ref[here, 2 * PAIR :]
        keys_turned = jnp.transpose(keys * scale)
        key_grad = jnp.zeros((rows, PAIR), F32)
        value_grad = jnp.zeros((rows, PAIR), F32)
        for head in range(2):
            part = slice(HEAD_DIM * head, HEAD_DIM * (head + 1))
            for low, high in ((start, start + rows), (start + rows, tokens)):
                if low == high:
                    continue
                scores = dot(keys, queries[head][low:high], 1, 1)
                if low == start:
                    scores = jnp.where(causal, scores, MASKED)
                probs = jnp.exp(scores - lse_ref[head : head + 1, low:high])
                grad_probs = dot(values, grads[head][low:high], 1, 1)
                grad_scores = (probs * (grad_probs - delta[head][:, low:high])).astype(BF16)
                value_grad = value_grad + dot(probs.astype(BF16), grads[head][low:high])
                key_grad = key_grad + dot(grad_scores, queries[head][low:high])
                turned = dot(keys_turned[part], grad_scores)
                if block == 0:
                    dq_ref[part, low:high] = turned
                else:
                    dq_ref[part, low:high] += turned
        result_ref[here, PAIR : 2 * PAIR] = key_grad.astype(BF16)
        result_ref[here, 2 * PAIR :] = value_grad.astype(BF16)
    result_ref[:, :PAIR] = jnp.transpose(dq_ref[...]).astype(BF16)

    result = result_ref[...]
    sums = jnp.sum(result.astype(F32), axis=0, keepdims=True)
    sums_ref[...] = sums
    rows_copy.wait()
    weight_grad = jnp.transpose(dot(result, rows_ref[...], 0, 0))
    out_weight_grad = jnp.transpose(dot(out, grad_ref[...], 0, 0))
    high = sums.astype(BF16)
    low = (sums - high.astype(F32)).astype(BF16)
    weight = weight_ref[...]
    shift = dot(high, weight, 1, 1) + dot(low, weight, 1, 1)
    gain = (to_row(weight.astype(F32) * weight_grad) - norm_ref[1:2, :] * shift) / norm_ref[0:1, :]
    vector_ref[0:1, :] = gain
    vector_ref[1:2, :] = shift
    wide = weight_grad.shape[1]
    if kind == "flat":
        whole_ref = refs[ties + 4]
        whole_ref[:, :wide] = weight_grad
        whole_ref[:, wide:] = out_weight_grad
        return
    target = refs[ties + 4] if kind == "whole" else product_ref
    count, shard = target.shape[:2]
    target[:, :, :wide] = weight_grad.reshape(count, shard, wide)
    target[:, :, wide:] = out_weight_grad.reshape(count, shard, PAIR)
    if kind == "whole":
        return
    kept_ref, away_ref = refs[ties + 4 : ties + 6]
    for block in range(count // 2):
        keep = scatter_block(info_ref, 0, block, False, count)
        send = scatter_block(info_ref, 0, block, True, count)
        start = 0
        if kind == "joined":
            start = before_ref.shape[2]
            kept_ref[block, :, :start] = before_ref[keep]
            away_ref[block, :, :start] = before_ref[send].astype(BF16)
        kept_ref[block, :, start:] = product_ref[keep]
        away_ref[block, :, start:] = product_ref[send].astype(BF16)


def feed_forward_kernel(
    info_ref,
    own_ref,
    other_ref,
    cot_own_ref,
    cot_other_ref,
    bias_ref,
    *refs,
    blocks,
    placed,
):
    weights, refs = refs[:2], refs[2:]
    terms_own_ref, terms_other_ref, back_own_ref, back_other_ref, sums_ref = refs[:5]
    refs = refs[5:]
    step = pl.program_id(0)
    own = step < blocks
    if placed:
        grad_fc_ref, grad_proj_ref = refs
        fc, proj = (ref[...] for ref in weights)
    else:
        kept_ref, away_ref, fc_ref, proj_ref, grad_fc_ref, grad_proj_ref, away_scratch, sems = refs
        count = fc_ref.shape[0]
        half = count // 2

        @pl.when(step == 0)
        def _():
            copies = []
            for number, target in enumerate((fc_ref, proj_ref)):
                for place in range(count):
                    source = weights[place // half].at[
                        place % half, :, pl.ds(number * target.shape[2], target.shape[2])
                    ]
                    copies.append(
                        pltpu.make_async_copy(
                            source,
                            target.at[gathered_owner(info_ref, place, count)],
                            sems.at[number * count + place],
                        )
                    )
                    copies[-1].start()
            for copy in copies:
                copy.wait()

        fc, proj = (ref[...].reshape(-1, ref.shape[2]) for ref in (fc_ref, proj_ref))

    @pl.when(step == 0)
    def _():
        sums_ref[...] = jnp.zeros_like(sums_ref)
        grad_fc_ref[...] = jnp.zeros_like(grad_fc_ref)
        grad_proj_ref[...] = jnp.zeros_like(grad_proj_ref)

    rows = jnp.where(own, own_ref[...], other_ref[...])
    cot = jnp.where(own, cot_own_ref[...], cot_other_ref[...])
    pre = dot(rows, fc) + bias_ref[...]
    slope = math.sqrt(2.0 / math.pi)
    square = pre * pre
    bent = jnp.tanh(slope * pre * (1.0 + 0.044715 * square))
    upper = 0.5 * (1.0 + bent)
    act = (pre * upper).astype(BF16)
    terms = dot(act, proj, 1, 1)
    grad_proj_ref[...] += dot(cot, act, 0, 0).reshape(grad_proj_ref.shape)
    derivative = upper + 0.5 * pre * (1.0 - bent * bent) * (
        slope * (1.0 + 3.0 * 0.044715 * square)
    )
    grad_pre = (dot(cot, proj) * derivative).astype(BF16)
    back = dot(grad_pre, fc, 1, 1)
    grad_fc_ref[...] += dot(rows, grad_pre, 0, 0).reshape(grad_fc_ref.shape)
    sums_ref[...] += jnp.sum(grad_pre.astype(F32), axis=0, keepdims=True)

    @pl.when(own)
    def _():
        terms_own_ref[...] = terms
        back_own_ref[...] = back

    @pl.when(jnp.logical_not(own))
    def _():
        terms_other_ref[...] = terms.astype(BF16)
        back_other_ref[...] = back.astype(BF16)

    if not placed:
        hidden = fc_ref.shape[2]

        @pl.when(step == 2 * blocks - 1)
        def _():
            copies = []
            for number, grad_ref in enumerate((grad_fc_ref, grad_proj_ref)):
                for block in range(half):
                    copies.append(
                        pltpu.make_async_copy(
                            grad_ref.at[scatter_block(info_ref, 0, block, False, count)],
                            kept_ref.at[block, :, pl.ds(number * hidden, hidden)],
                            sems.at[number * half + block],
                        )
                    )
                    copies[-1].start()
            for number, grad_ref in enumerate((grad_fc_ref, grad_proj_ref)):
                for block in range(half):
                    away_scratch[block, :, number * hidden : (number + 1) * hidden] = grad_ref[
                        scatter_block(info_ref, 0, block, True, count)
                    ].astype(BF16)
            send = pltpu.make_async_copy(away_scratch, away_ref, sems.at[2 * half])
            send.start()
            for copy in copies + [send]:
                copy.wait()


ANY_SPEC = pl.BlockSpec(memory_space=pl.ANY)
TOKEN_SHAPE = jax.ShapeDtypeStruct((1, 1), F32)
TOKEN_SPEC = pl.BlockSpec((1, 1), lambda *_: (0, 0))


def attend_forward(pair, normed, weight, bias, ties):
    halves = isinstance(normed, tuple)
    tokens = 2 * normed[1].shape[0] if halves else normed.shape[0]
    features, columns = weight.shape
    every = pl.BlockSpec((tokens, features), lambda: (0, 0))
    in_specs = [
        pl.BlockSpec((features, columns), lambda: (0, 0)),
        pl.BlockSpec((1, columns), lambda: (0, 0)),
    ]
    out_specs = [
        pl.BlockSpec((tokens, columns), lambda: (0, 0)),
        pl.BlockSpec((tokens, PAIR), lambda: (0, 0)),
        pl.BlockSpec((2, tokens), lambda: (0, 0)),
        pl.BlockSpec((1, 1), lambda: (0, 0)),
    ]
    out_shape = [
        jax.ShapeDtypeStruct((tokens, columns), BF16),
        jax.ShapeDtypeStruct((tokens, PAIR), BF16),
        jax.ShapeDtypeStruct((2, tokens), F32),
        TOKEN_SHAPE,
    ]
    if halves:
        half = pl.BlockSpec((tokens // 2, features), lambda: (0, 0))
        in_specs += [pl.BlockSpec(memory_space=pltpu.SMEM), half, half]
        out_specs = [every] + out_specs
        out_shape = [jax.ShapeDtypeStruct((tokens, features), BF16)] + out_shape
    else:
        in_specs += [every]
    in_specs += [ANY_SPEC] * len(ties)
    out = pl.pallas_call(
        functools.partial(forward_kernel, rows=512, halves=halves),
        in_specs=in_specs,
        out_specs=out_specs,
        out_shape=out_shape,
        compiler_params=pltpu.CompilerParams(vmem_limit_bytes=VMEM_BYTES),
        cost_estimate=SMALL_COST,
        name=f"attend_forward_{pair}",
    )(weight, bias, *(normed if halves else (normed,)), *ties)
    return out[0] if halves else normed, *out[-4:-1], out[-1].reshape(())


def attend_backward(
    pair, kind, projected, heads, lse, weight, info, own, other, normed, out_weight, norm, ties
):
    tokens, columns = projected.shape
    features = normed.shape[1]
    count = lax.axis_size("dp")
    shard = features // count
    fixed = lambda shape: pl.BlockSpec(shape, lambda _: (0,) * len(shape))
    scalars = pl.BlockSpec(memory_space=pltpu.SMEM)
    out_shape = [
        jax.ShapeDtypeStruct((tokens, columns), BF16),
        jax.ShapeDtypeStruct((1, columns), F32),
        jax.ShapeDtypeStruct((2, features), F32),
        TOKEN_SHAPE,
    ]
    wide = 4 * PAIR
    product = pltpu.VMEM((8, 128), F32)
    tie_specs = [ANY_SPEC] * len(ties)
    if shard % 16:
        inner = "flat"
        out_shape += [jax.ShapeDtypeStruct((features, wide), F32)]
    elif kind == "whole":
        inner = kind
        out_shape += [jax.ShapeDtypeStruct((count, shard, wide), F32)]
    else:
        inner = kind
        width = wide
        if kind == "joined":
            width += ties[0].shape[2]
            tie_specs[0] = fixed(ties[0].shape)
        out_shape += [
            jax.ShapeDtypeStruct((count // 2, shard, width), held) for held in (F32, BF16)
        ]
        product = pltpu.VMEM((count, shard, wide), F32)
    out = pl.pallas_call(
        functools.partial(backward_kernel, rows=256, ties=len(ties), kind=inner),
        grid=(1,),
        in_specs=[
            scalars,
            fixed(projected.shape),
            fixed(heads.shape),
            fixed(lse.shape),
            ANY_SPEC,
            ANY_SPEC,
            ANY_SPEC,
            fixed(weight.shape),
            pl.BlockSpec((features, PAIR), lambda _: (0, pair)),
            fixed(norm.shape),
        ]
        + tie_specs,
        out_specs=[fixed(result.shape) for result in out_shape],
        out_shape=out_shape,
        scratch_shapes=[
            pltpu.VMEM((tokens, features), BF16),
            pltpu.VMEM((PAIR, tokens), F32),
            product,
            pltpu.VMEM((tokens, features), BF16),
            pltpu.SemaphoreType.DMA((3,)),
        ],
        compiler_params=pltpu.CompilerParams(vmem_limit_bytes=VMEM_BYTES),
        cost_estimate=SMALL_COST,
        name=f"attend_backward_{pair}",
    )(info, projected, heads, lse, own, other, normed, weight, out_weight, norm, *ties)
    if kind == "whole":
        gradient = out[4]
    elif shard % 16:
        gradient = Scatter(out[4] if kind == "split" else jnp.concatenate([ties[0], out[4]], axis=1))
    else:
        gradient = Scatter(out[4], out[5])
    return out[0], out[1], out[2], out[3], gradient


def feed_forward(info, own, other, cot_own, cot_other, bias, gather):
    tokens, features = own.shape
    hidden = bias.shape[0]
    block = 512
    blocks = tokens // block
    count = lax.axis_size("dp")
    shard = features // count
    placed = shard % 16 != 0
    first = pl.BlockSpec((block, features), lambda i: (jnp.minimum(i, blocks - 1), 0))
    second = pl.BlockSpec((block, features), lambda i: (jnp.maximum(i - blocks, 0), 0))
    out_specs = [first, second, first, second, pl.BlockSpec((1, hidden), lambda i: (0, 0))]
    out_shape = [
        jax.ShapeDtypeStruct((tokens, features), kind) for kind in (F32, BF16, F32, BF16)
    ] + [jax.ShapeDtypeStruct((1, hidden), F32)]
    scratch = []
    weights = [gather.held, gather.got]
    weight_specs = [ANY_SPEC] * 2
    if placed:
        both = gather.result()
        weights = [both[:, :hidden], both[:, hidden:]]
        weight_specs = [pl.BlockSpec((features, hidden), lambda i: (0, 0))] * 2
        out_specs += [pl.BlockSpec((features, hidden), lambda i: (0, 0))] * 2
        out_shape += [jax.ShapeDtypeStruct((features, hidden), F32)] * 2
    else:
        out_specs += [ANY_SPEC] * 2
        out_shape += [
            jax.ShapeDtypeStruct((count // 2, shard, 2 * hidden), kind) for kind in (F32, BF16)
        ]
        scratch = [
            pltpu.VMEM((count, shard, hidden), BF16),
            pltpu.VMEM((count, shard, hidden), BF16),
            pltpu.VMEM((count, shard, hidden), F32),
            pltpu.VMEM((count, shard, hidden), F32),
            pltpu.VMEM((count // 2, shard, 2 * hidden), BF16),
            pltpu.SemaphoreType.DMA((2 * count,)),
        ]
    out = pl.pallas_call(
        functools.partial(feed_forward_kernel, blocks=blocks, placed=placed),
        grid=(2 * blocks,),
        in_specs=[
            pl.BlockSpec(memory_space=pltpu.SMEM),
            first,
            second,
            first,
            second,
            pl.BlockSpec((1, hidden), lambda i: (0, 0)),
        ]
        + weight_specs,
        out_specs=out_specs,
        out_shape=out_shape,
        scratch_shapes=scratch,
        compiler_params=pltpu.CompilerParams(vmem_limit_bytes=VMEM_BYTES),
        cost_estimate=SMALL_COST,
        name="feed_forward",
    )(info, own, other, cot_own, cot_other, bias.reshape(1, hidden), *weights)
    if placed:
        return (*out[:5], Scatter(jnp.concatenate(out[5:], axis=1)))
    return (*out[:5], Scatter(*out[5:]))


def block_call(kernel, grid, in_specs, operands, out, scratch=(), name=None, ties=()):
    return pl.pallas_call(
        kernel,
        grid=grid,
        in_specs=list(in_specs) + [ANY_SPEC] * len(ties),
        out_specs=[pl.BlockSpec(block, index) for _, _, block, index in out],
        out_shape=[jax.ShapeDtypeStruct(shape, kind) for shape, kind, _, _ in out],
        scratch_shapes=list(scratch),
        compiler_params=pltpu.CompilerParams(vmem_limit_bytes=VMEM_BYTES),
        cost_estimate=SMALL_COST,
        name=name,
    )(*operands, *ties)


def whole_spec(array):
    return pl.BlockSpec(array.shape, lambda *_: (0,) * array.ndim)


def out_product_kernel(info_ref, weight_ref, *refs):
    heads_refs, (own_ref, other_ref) = refs[:-2], refs[-2:]
    half = own_ref.shape[0]
    for target, at in ((other_ref, 1 - info_ref[1]), (own_ref, info_ref[1])):
        here = pl.ds(pl.multiple_of(at * half, half), half)
        heads = jnp.concatenate([ref[here, :] for ref in heads_refs], axis=1)
        target[...] = dot(heads, weight_ref[...], 1, 1).astype(target.dtype)


def out_product(info, weight, heads):
    half = heads[0].shape[0] // 2
    width = weight.shape[0]
    return block_call(
        out_product_kernel,
        (1,),
        [pl.BlockSpec(memory_space=pltpu.SMEM), whole_spec(weight)] + [whole_spec(h) for h in heads],
        [info, weight, *heads],
        [((half, width), kind, (half, width), lambda _: (0, 0)) for kind in (F32, BF16)],
        name="out_product",
    )


def back_product_kernel(info_ref, *refs, pairs):
    own_ref, other_ref = refs[-2:]
    half = own_ref.shape[0]
    for target, at in ((other_ref, 1 - info_ref[1]), (own_ref, info_ref[1])):
        here = pl.ds(pl.multiple_of(at * half, half), half)
        total = 0.0
        for result, weight in zip(refs[:pairs], refs[pairs : 2 * pairs]):
            total = total + dot(result[here, :], weight[...], 1, 1)
        target[...] = total.astype(target.dtype)


def back_product(info, results, weights, ties):
    half = results[0].shape[0] // 2
    width = weights[0].shape[0]
    return block_call(
        functools.partial(back_product_kernel, pairs=len(results)),
        (1,),
        [pl.BlockSpec(memory_space=pltpu.SMEM)] + [whole_spec(a) for a in (*results, *weights)],
        [info, *results, *weights],
        [((half, width), kind, (half, width), lambda _: (0, 0)) for kind in (F32, BF16)],
        name="back_product",
        ties=ties,
    )


def middle_kernel(hidden_ref, own_ref, other_ref, bias_ref, norm_ref, *refs):
    middle_ref, normed_ref = refs[-2:]
    middle = (
        hidden_ref[...].astype(F32) + (own_ref[...] + other_ref[...].astype(F32)) + bias_ref[...]
    )
    middle_ref[...] = middle
    normed_ref[...] = norm_layer(middle, norm_ref[0:1, :], norm_ref[1:2, :]).astype(BF16)


def middle_norm(hidden, own, other, bias, norm, ties):
    rows, width = hidden.shape
    tile = pl.BlockSpec((256, width), lambda i: (i, 0))
    return block_call(
        middle_kernel,
        (rows // 256,),
        [tile, tile, tile, whole_spec(bias), whole_spec(norm)],
        [hidden, own, other, bias, norm],
        [(hidden.shape, kind, (256, width), lambda i: (i, 0)) for kind in (F32, BF16)],
        name="middle_norm",
        ties=ties,
    )


def norm_slope(rows, grad, gain):
    centred = rows - jnp.mean(rows, axis=-1, keepdims=True)
    scale = lax.rsqrt(jnp.mean(centred * centred, axis=-1, keepdims=True) + 1e-05)
    normalised = centred * scale
    scaled = grad * gain
    back = scale * (
        scaled
        - jnp.mean(scaled, axis=-1, keepdims=True)
        - normalised * jnp.mean(scaled * normalised, axis=-1, keepdims=True)
    )
    return normalised, back


def middle_back_kernel(
    middle_ref, own_ref, other_ref, cot_ref, norm_ref, grad_ref, attn_ref, sums_ref
):
    @pl.when(pl.program_id(0) == 0)
    def _():
        sums_ref[...] = jnp.zeros_like(sums_ref)

    back = own_ref[...] + other_ref[...].astype(F32)
    cot = cot_ref[...].astype(F32)
    normalised, through = norm_slope(middle_ref[...], back, norm_ref[0:1, :])
    grad = cot + through
    attn = grad.astype(BF16)
    grad_ref[...] = grad
    attn_ref[...] = attn
    for row, values in enumerate((back * normalised, back, attn.astype(F32), cot)):
        sums_ref[row : row + 1, :] += jnp.sum(values, axis=0, keepdims=True)


def middle_back(middle, own, other, cot, norm):
    rows, width = middle.shape
    tile = pl.BlockSpec((256, width), lambda i: (i, 0))
    return block_call(
        middle_back_kernel,
        (rows // 256,),
        [tile, tile, tile, tile, whole_spec(norm)],
        [middle, own, other, cot, norm],
        [(middle.shape, kind, (256, width), lambda i: (i, 0)) for kind in (F32, BF16)]
        + [((8, width), F32, (8, width), lambda i: (0, 0))],
        name="middle_back",
    )


def first_back_kernel(hidden_ref, own_ref, other_ref, grad_ref, norm_ref, *refs):
    result_ref = refs[-1]
    back = own_ref[...] + other_ref[...].astype(F32)
    _, through = norm_slope(hidden_ref[...].astype(F32), back, norm_ref[0:1, :])
    result_ref[...] = (grad_ref[...] + through).astype(BF16)


def first_back(hidden, own, other, grad, norm, ties):
    rows, width = hidden.shape
    tile = pl.BlockSpec((256, width), lambda i: (i, 0))
    return block_call(
        first_back_kernel,
        (rows // 256,),
        [tile, tile, tile, tile, whole_spec(norm)],
        [hidden, own, other, grad, norm],
        [(hidden.shape, BF16, (256, width), lambda i: (i, 0))],
        name="first_back",
        ties=ties,
    )[0]


def vectors_kernel(early_ref, hidden_ref, *refs, pairs):
    out_ref = refs[-1]
    width = out_ref.shape[1]
    out_ref[...] = jnp.zeros_like(out_ref)
    out_ref[0:2, :] = sum(ref[...] for ref in refs[:pairs])
    out_ref[2:6, :] = early_ref[0:4, :]
    wide = hidden_ref.shape[1] // width
    for row in range(wide):
        out_ref[6 + row : 7 + row, :] = hidden_ref[:, row * width : (row + 1) * width]
    for pair, ref in enumerate(refs[pairs : 2 * pairs]):
        start = pair * PAIR
        out_ref[6 + wide : 7 + wide, start : start + PAIR] = ref[:, :PAIR]
        start += pairs * PAIR
        out_ref[6 + wide : 7 + wide, start : start + PAIR] = ref[:, 2 * PAIR :]


def vectors_of(early, hidden, parts, sums, ties):
    operands = [early, hidden, *parts, *sums]
    return block_call(
        functools.partial(vectors_kernel, pairs=len(parts)),
        (1,),
        [whole_spec(a) for a in operands],
        operands,
        [((16, early.shape[1]), F32, (16, early.shape[1]), lambda _: (0, 0))],
        name="vectors",
        ties=ties,
    )[0]


def join_gathered_kernel(token_ref, held_ref, got_ref, *refs):
    @pl.when(pl.program_id(0) == 0)
    def _():
        refs[-1][...] = held_ref[...]

    @pl.when(pl.program_id(0) == 1)
    def _():
        refs[-1][...] = got_ref[...]


def join_gathered(held, got, token, ties):
    if held.shape[1] % 16 or token is None:
        return jnp.concatenate([held, got], axis=0)
    count, rows, columns = held.shape
    token = token.reshape(1, 1)
    return block_call(
        join_gathered_kernel,
        (2,),
        [pl.BlockSpec(memory_space=pltpu.SMEM), whole_spec(held), whole_spec(got)],
        [token, held, got],
        [((2 * count, rows, columns), held.dtype, held.shape, lambda i: (i, 0, 0))],
        name="join_gathered",
        ties=ties,
    )[0]


def exchange(block, bits):
    count = lax.axis_size("dp")
    width = lax.axis_size("tensor")
    pairs = [
        (i * width + t, (i ^ (1 << bits[t % 2])) * width + t)
        for i in range(count)
        for t in range(width)
    ]
    return lax.ppermute(block, ("dp", "tensor"), pairs)


def swap(block):
    count = lax.axis_size("tensor")
    return lax.ppermute(block, "tensor", [(i, count - 1 - i) for i in range(count)])


class Gather:
    def __init__(self, shard):
        self.orders = list(zip(*gather_orders(lax.axis_size("dp"))))
        self.held = shard[None]
        self.step = 0
        self.got = exchange(self.held, self.orders[0])

    def advance(self, token=None, ties=()):
        self.step += 1
        if self.step < len(self.orders):
            self.held = join_gathered(self.held, self.got, token, ties)
            self.got = exchange(self.held, self.orders[self.step])
        return self

    def result(self, token=None):
        while self.step < len(self.orders) - 1:
            self.advance()
        return place_rows(place_info(), self.held, self.got, token)


def place_kernel(info_ref, token_ref, held_ref, got_ref, out_ref, sems):
    half = held_ref.shape[0]
    copies = []
    for place in range(2 * half):
        source = held_ref.at[place] if place < half else got_ref.at[place - half]
        owner = gathered_owner(info_ref, place, 2 * half)
        copies.append(pltpu.make_async_copy(source, out_ref.at[owner], sems.at[place]))
        copies[-1].start()
    for copy in copies:
        copy.wait()


def place_rows(info, held, got, token=None):
    half, rows, columns = held.shape
    count = 2 * half
    if rows % 16:
        owners = gathered_owner(info, jnp.arange(count, dtype=jnp.int32), count)
        placed = jnp.concatenate([held, got], axis=0)[jnp.argsort(owners)]
        return placed.reshape(count * rows, columns)
    placed = pl.pallas_call(
        place_kernel,
        in_specs=[pl.BlockSpec(memory_space=pltpu.SMEM)] * 2 + [ANY_SPEC] * 2,
        out_specs=pl.BlockSpec(memory_space=pltpu.VMEM),
        out_shape=jax.ShapeDtypeStruct((count, rows, columns), BF16),
        scratch_shapes=[pltpu.SemaphoreType.DMA((count,))],
        compiler_params=pltpu.CompilerParams(vmem_limit_bytes=16 * 1024 * 1024),
        cost_estimate=SMALL_COST,
        name="place_rows",
    )(info, jnp.zeros((1, 1), F32) if token is None else token.reshape(1, 1), held, got)
    return placed.reshape(count * rows, columns)


def join_kernel(info_ref, token_ref, keep_ref, send_ref, got_keep_ref, got_send_ref, *refs):
    kept_ref, away_ref = refs[-2:]
    kept_ref[...] = keep_ref[...] + got_keep_ref[...].astype(F32)
    away_ref[...] = (send_ref[...] + got_send_ref[...].astype(F32)).astype(BF16)


def join_halves(info, step, held, got, token, ties):
    count, rows, columns = held.shape
    half = count // 2
    size = lax.axis_size("dp")

    def at(sent):
        return pl.BlockSpec(
            (1, rows, columns), lambda i, info: (scatter_block(info, step, i, sent, size), 0, 0)
        )

    result = pl.BlockSpec((1, rows, columns), lambda i, info: (i, 0, 0))
    return pl.pallas_call(
        join_kernel,
        grid_spec=pltpu.PrefetchScalarGridSpec(
            num_scalar_prefetch=1,
            grid=(half,),
            in_specs=[pl.BlockSpec(memory_space=pltpu.SMEM), at(False), at(True), at(False), at(True)]
            + [ANY_SPEC] * len(ties),
            out_specs=[result, result],
        ),
        out_shape=[jax.ShapeDtypeStruct((half, rows, columns), kind) for kind in (F32, BF16)],
        compiler_params=pltpu.CompilerParams(vmem_limit_bytes=16 * 1024 * 1024),
        cost_estimate=SMALL_COST,
        name="join_halves",
    )(info, jnp.zeros((1, 1), F32) if token is None else token, held, held, got, got, *ties)


class Scatter:
    def __init__(self, whole, away=None):
        self.orders = list(zip(*scatter_orders(lax.axis_size("dp"))))
        self.step = 0
        if away is None:
            count = lax.axis_size("dp")
            self.split(whole.reshape(count, whole.shape[0] // count, whole.shape[1]))
        else:
            self.kept, self.away = whole, away
        self.got = exchange(self.away, self.orders[0])

    def split(self, held):
        count = lax.axis_size("dp")
        blocks = jnp.arange(held.shape[0] // 2, dtype=jnp.int32)
        keep, send = (
            scatter_block(place_info(), self.step, blocks, sent, count) for sent in (False, True)
        )
        self.kept = jnp.take(held, keep, axis=0)
        self.away = jnp.take(held, send, axis=0).astype(BF16)

    def advance(self, token=None, ties=()):
        self.step += 1
        if self.kept.shape[1] % 16:
            self.split(self.kept + self.got.astype(F32))
        else:
            self.kept, self.away = join_halves(
                place_info(), self.step, self.kept, self.got, token, ties
            )
        self.got = exchange(self.away, self.orders[self.step])

    def result(self):
        while self.step < len(self.orders) - 1:
            self.advance()
        return (self.kept + self.got.astype(F32))[0]


class VectorSum:
    def __init__(self, rows, both):
        self.rows, self.both, self.bit = rows, both, 0

    def advance(self, steps=1):
        for _ in range(steps):
            if self.bit < bits_of(lax.axis_size("dp")):
                self.rows = self.rows + exchange(self.rows, (self.bit, self.bit))
                self.bit += 1
        return self.rows

    def result(self):
        self.advance(bits_of(lax.axis_size("dp")))
        return self.rows[: self.both] + swap(self.rows[: self.both]), self.rows[self.both :]


def per_device(
    hidden_in,
    first_gain,
    first_shift,
    qkv_weight,
    qv_bias,
    out_weight,
    out_bias,
    second_gain,
    second_shift,
    fc_weight,
    fc_bias,
    proj_weight,
    proj_bias,
    cotangent,
):
    width = hidden_in.shape[1]
    shard_rows = qkv_weight.shape[0]
    head_width = qkv_weight.shape[2]
    pairs = head_width // PAIR
    columns = 3 * PAIR

    by_pair = qkv_weight.reshape(shard_rows, 3, pairs, PAIR).swapaxes(1, 2)
    by_pair = by_pair.reshape(shard_rows, pairs * columns)
    early = pairs - 1
    first_gather = Gather(by_pair[:, : early * columns])
    rest_gather = Gather(jnp.concatenate([by_pair[:, early * columns :], out_weight], axis=1))
    ff_gather = Gather(jnp.concatenate([fc_weight, proj_weight], axis=1))

    rows_first = hidden_in.astype(F32)
    row_mean = jnp.mean(rows_first, axis=-1, keepdims=True)
    centred = rows_first - row_mean
    first_rsqrt = lax.rsqrt(jnp.mean(centred * centred, axis=-1, keepdims=True) + 1e-05)
    normed_piece = (centred * first_rsqrt * first_gain + first_shift).astype(BF16)
    info = place_info()
    normed_first = (info, normed_piece, swap(normed_piece))
    cot_other = swap(cotangent)

    bias_parts = jnp.stack([qv_bias[0], jnp.zeros_like(qv_bias[0]), qv_bias[1]])
    bias_cols = bias_parts.reshape(3, pairs, PAIR).swapaxes(0, 1).reshape(pairs, 1, columns)
    ff_gather.advance()
    weights = first_gather.result()
    qkv_weights = [weights[:, p * columns : (p + 1) * columns] for p in range(early)]
    projected, heads, lses = [], [], []
    for pair in range(pairs):
        normed_first, columns_out, heads_out, lse, token = attend_forward(
            pair,
            normed_first,
            qkv_weights[pair],
            bias_cols[pair],
            [ff_gather.held] if pair else [],
        )
        projected.append(columns_out)
        heads.append(heads_out)
        lses.append(lse)
        if pair == early - 1:
            rest = rest_gather.result(token)
            qkv_weights.append(rest[:, :columns])
            full_out = rest[:, columns:]
        if pair < pairs - 1:
            ff_gather.advance(token)

    attn_own, attn_other = out_product(info, full_out, heads)
    norm_second = jnp.stack([second_gain, second_shift])
    middle, normed_own = middle_norm(
        hidden_in,
        attn_own,
        swap(attn_other),
        out_bias[None],
        norm_second,
        [],
    )
    normed_other = swap(normed_own)
    terms_own, terms_other, back_own, back_other, sum_fc, ff_sum = feed_forward(
        info, normed_own, normed_other, cotangent, cot_other, fc_bias, ff_gather
    )
    back_other = swap(back_other)
    terms_other = swap(terms_other)
    block_out = (middle + (terms_own + terms_other.astype(F32)) + proj_bias).astype(BF16)
    grad_middle, grad_attn, sums_second = middle_back(
        middle, back_own, back_other, cotangent, norm_second
    )
    grad_attn_other = swap(grad_attn)
    hidden = fc_weight.shape[1]
    norm_first = jnp.stack([first_gain, first_shift])
    shared = (info, grad_attn, grad_attn_other, normed_first, full_out, norm_first)
    kinds = ["split"] + ["whole"] * (pairs - 2) + ["joined"]
    results, column_sums, vector_parts = [], [], []
    first_sum = rest_sum = whole = None
    for pair in range(pairs):
        ties = [] if whole is None else [whole]
        if pair:
            ties += [ff_sum.away, first_sum.away]
        result, sums, vector, token, gradient = attend_backward(
            pair,
            kinds[pair],
            projected[pair],
            heads[pair],
            lses[pair],
            qkv_weights[pair],
            *shared,
            ties,
        )
        results.append(result)
        column_sums.append(sums)
        vector_parts.append(vector)
        if pair < pairs - 1:
            ff_sum.advance(token)
            if pair:
                first_sum.advance(token)
        if pair == 0:
            first_sum = gradient
        elif pair == pairs - 1:
            rest_sum = gradient
        else:
            whole = gradient
    back_own, back_other = back_product(info, results, qkv_weights, [])
    ff_sum.advance(ties=(back_other,))
    first_sum.advance(ties=(back_other,))
    rest_sum.advance(ties=(ff_sum.away, first_sum.away))
    grad_hidden = first_back(
        hidden_in, back_own, swap(back_other), grad_middle, norm_first, [rest_sum.away]
    )
    vector_sum = VectorSum(
        vectors_of(sums_second, sum_fc, vector_parts, column_sums, [rest_sum.away]), 6
    )
    first_sum.advance(ties=(rest_sum.away,))
    rest_sum.advance(ties=(first_sum.away, vector_sum.advance()))
    rest_sum.advance(ties=(vector_sum.advance(2), grad_hidden))
    own_heads = jnp.concatenate([first_sum.result(), rest_sum.result()], axis=1).reshape(
        shard_rows, pairs, 4, PAIR
    )
    own_outw = own_heads[:, :, 3].reshape(shard_rows, head_width)
    own_qkv = own_heads[:, :, :3].swapaxes(1, 2).reshape(shard_rows, 3, head_width)
    own_ff = ff_sum.result()
    sums, own_sums = vector_sum.result()
    hidden_rows = hidden // width
    return (
        block_out,
        grad_hidden,
        sums[0],
        sums[1],
        own_qkv,
        own_sums[hidden_rows].reshape(2, head_width),
        own_outw,
        sums[4],
        sums[2],
        sums[3],
        own_ff[:, :hidden],
        own_sums[:hidden_rows].reshape(hidden),
        own_ff[:, hidden:],
        sums[5],
    )


def solution(mesh):
    placed = (
        P(("dp", "tensor"), None),
        P(),
        P(),
        P("dp", None, "tensor"),
        P(None, "tensor"),
        P("dp", "tensor"),
        P(),
        P(),
        P(),
        P("dp", "tensor"),
        P("tensor"),
        P("dp", "tensor"),
        P(),
        P(("dp", "tensor"), None),
    )
    return jax.shard_map(
        per_device,
        mesh=mesh,
        in_specs=placed,
        out_specs=(
            P(("dp", "tensor"), None),
            P(("dp", "tensor"), None),
            P(),
            P(),
            P("dp", None, "tensor"),
            P(None, "tensor"),
            P("dp", "tensor"),
            P(),
            P(),
            P(),
            P("dp", "tensor"),
            P("tensor"),
            P("dp", "tensor"),
            P(),
        ),
        check_vma=False,
    )
```

```python
import functools
import math

import jax
import jax.numpy as jnp
from jax import lax
from jax.experimental import pallas as pl
from jax.experimental.pallas import tpu as pltpu
from jax.sharding import PartitionSpec as P

HEAD_DIM = 64
SEQ_LEN = 2048
PAIR = 2 * HEAD_DIM
F32 = jnp.float32
BF16 = jnp.bfloat16
VMEM_BYTES = 56 * 1024 * 1024
MASKED = -1e30
SMALL_COST = pl.CostEstimate(flops=1, bytes_accessed=1, transcendentals=0)


def norm_layer(rows_in, gain_vec, shift_vec):
    row_mean = jnp.mean(rows_in, axis=-1, keepdims=True)
    centred = rows_in - row_mean
    variance = jnp.mean(centred * centred, axis=-1, keepdims=True)
    return centred * lax.rsqrt(variance + 1e-05) * gain_vec + shift_vec


def dot(left, right, left_axis=1, right_axis=0):
    return lax.dot_general(
        left, right, (((left_axis,), (right_axis,)), ((), ())), preferred_element_type=F32
    )


def bits_of(count):
    return count.bit_length() - 1


def gather_orders(count):
    even = list(range(bits_of(count)))[::-1]
    odd = even[:-2] + [0, 1]
    if len(even) == 4:
        odd = [2, 3, 0, 1]
    return even, odd


def scatter_orders(count):
    bits = list(range(bits_of(count)))
    return bits, [1, 0] + bits[2:]


def place_info():
    return jnp.stack([lax.axis_index("dp"), lax.axis_index("tensor")]).astype(jnp.int32)


def gathered_owner(info, place, count):
    even, odd = (
        sum(((place >> step) & 1) << bit for step, bit in enumerate(order))
        for order in gather_orders(count)
    )
    return jnp.where(info[1] % 2 == 0, even, odd) ^ info[0]


def scatter_block(info, step, block, sent, count):
    found = []
    for order in scatter_orders(count):
        bit = order[step]
        at = sorted(order[step:]).index(bit)
        own = ((info[0] >> bit) & 1) ^ (1 if sent else 0)
        found.append(((block >> at) << (at + 1)) | (own << at) | (block & ((1 << at) - 1)))
    return jnp.where(info[1] % 2 == 0, found[0], found[1])


def forward_kernel(weight_ref, bias_ref, *refs, rows, halves):
    if halves:
        info_ref, own_ref, other_ref = refs[:3]
        normed_ref, qkv_ref, out_ref, lse_ref, token_ref = refs[-5:]
        half = own_ref.shape[0]
        normed_ref[pl.ds(pl.multiple_of(info_ref[1] * half, half), half), :] = own_ref[...]
        normed_ref[pl.ds(pl.multiple_of((1 - info_ref[1]) * half, half), half), :] = other_ref[...]
    else:
        normed_ref = refs[0]
        qkv_ref, out_ref, lse_ref, token_ref = refs[-4:]
    token_ref[...] = jnp.zeros_like(token_ref)
    qkv_ref[...] = (dot(normed_ref[...], weight_ref[...]) + bias_ref[...]).astype(BF16)
    lane = lax.broadcasted_iota(jnp.int32, (1, PAIR), 1)
    mine = [lane < HEAD_DIM, lane >= HEAD_DIM]
    causal = lax.broadcasted_iota(jnp.int32, (rows, rows), 1) <= lax.broadcasted_iota(
        jnp.int32, (rows, rows), 0
    )
    zero = jnp.zeros((), BF16)
    one = jnp.ones((), BF16)
    scale = jnp.asarray(1.0 / math.sqrt(HEAD_DIM), BF16)
    keys = qkv_ref[:, PAIR : 2 * PAIR]
    values = qkv_ref[:, 2 * PAIR :]
    values_one = [jnp.where(lanes, values, one) for lanes in mine]
    for block in range(SEQ_LEN // rows):
        start = block * rows
        here = pl.ds(start, rows)
        queries = qkv_ref[here, :PAIR] * scale
        halves = []
        for head in range(2):
            query = jnp.where(mine[head], queries, zero)
            near = jnp.where(causal, dot(query, keys[start : start + rows], 1, 1), MASKED)
            top = jnp.max(near, axis=1, keepdims=True)
            if block:
                far = dot(query, keys[:start], 1, 1)
                top = jnp.maximum(top, jnp.max(far, axis=1, keepdims=True))
                far = jnp.exp(far - top).astype(BF16)
            near = jnp.exp(near - top).astype(BF16)
            weighted = dot(near, values_one[head][start : start + rows])
            if block:
                weighted = weighted + dot(far, values_one[head][:start])
            total = pltpu.roll(weighted, HEAD_DIM, 1)
            halves.append(weighted / total)
            lse = top + jnp.log(jnp.where(mine[head], total, weighted))
            lse_ref[head : head + 1, here] = jnp.transpose(lse)[0:1]
        out_ref[here, :] = jnp.where(mine[0], halves[0], halves[1]).astype(BF16)


def to_row(columns):
    folded = sum(columns[:, c : c + 128] for c in range(0, columns.shape[1], 128))
    return jnp.sum(jnp.transpose(folded), axis=0, keepdims=True)


def backward_kernel(
    info_ref,
    qkv_ref,
    heads_ref,
    lse_ref,
    own_ref,
    other_ref,
    normed_ref,
    weight_ref,
    out_weight_ref,
    norm_ref,
    *refs,
    rows,
    ties,
    kind,
):
    before_ref = refs[0]
    result_ref, sums_ref, vector_ref, token_ref = refs[ties : ties + 4]
    grad_ref, dq_ref, product_ref, rows_ref, sems = refs[-5:]
    token_ref[...] = jnp.zeros_like(token_ref)
    tokens = qkv_ref.shape[0]
    part = own_ref.shape[0]
    own_rows = pl.ds(pl.multiple_of(info_ref[1] * part, part), part)
    other_rows = pl.ds(pl.multiple_of((1 - info_ref[1]) * part, part), part)
    own_copy = pltpu.make_async_copy(own_ref, grad_ref.at[own_rows, :], sems.at[0])
    other_copy = pltpu.make_async_copy(other_ref, grad_ref.at[other_rows, :], sems.at[1])
    rows_copy = pltpu.make_async_copy(normed_ref, rows_ref, sems.at[2])
    own_copy.start()
    other_copy.start()
    rows_copy.start()
    own_copy.wait()
    other_copy.wait()

    lane = lax.broadcasted_iota(jnp.int32, (1, PAIR), 1)
    mine = [lane < HEAD_DIM, lane >= HEAD_DIM]
    causal = lax.broadcasted_iota(jnp.int32, (rows, rows), 0) <= lax.broadcasted_iota(
        jnp.int32, (rows, rows), 1
    )
    zero = jnp.zeros((), BF16)
    scale = jnp.asarray(1.0 / math.sqrt(HEAD_DIM), BF16)
    grad = dot(grad_ref[...], out_weight_ref[...]).astype(BF16)
    out = heads_ref[...]
    queries = [jnp.where(lanes, qkv_ref[:, :PAIR], zero) * scale for lanes in mine]
    grads = [jnp.where(lanes, grad, zero) for lanes in mine]
    product = jnp.transpose(grad.astype(F32) * out.astype(F32))
    delta = [
        jnp.sum(product[:HEAD_DIM], axis=0, keepdims=True),
        jnp.sum(product[HEAD_DIM:], axis=0, keepdims=True),
    ]
    for block in range(tokens // rows):
        start = block * rows
        here = pl.ds(start, rows)
        keys = qkv_ref[here, PAIR : 2 * PAIR]
        values = qkv_ref[here, 2 * PAIR :]
        keys_turned = jnp.transpose(keys * scale)
        key_grad = jnp.zeros((rows, PAIR), F32)
        value_grad = jnp.zeros((rows, PAIR), F32)
        for head in range(2):
            part = slice(HEAD_DIM * head, HEAD_DIM * (head + 1))
            for low, high in ((start, start + rows), (start + rows, tokens)):
                if low == high:
                    continue
                scores = dot(keys, queries[head][low:high], 1, 1)
                if low == start:
                    scores = jnp.where(causal, scores, MASKED)
                probs = jnp.exp(scores - lse_ref[head : head + 1, low:high])
                grad_probs = dot(values, grads[head][low:high], 1, 1)
                grad_scores = (probs * (grad_probs - delta[head][:, low:high])).astype(BF16)
                value_grad = value_grad + dot(probs.astype(BF16), grads[head][low:high])
                key_grad = key_grad + dot(grad_scores, queries[head][low:high])
                turned = dot(keys_turned[part], grad_scores)
                if block == 0:
                    dq_ref[part, low:high] = turned
                else:
                    dq_ref[part, low:high] += turned
        result_ref[here, PAIR : 2 * PAIR] = key_grad.astype(BF16)
        result_ref[here, 2 * PAIR :] = value_grad.astype(BF16)
    result_ref[:, :PAIR] = jnp.transpose(dq_ref[...]).astype(BF16)

    result = result_ref[...]
    sums = jnp.sum(result.astype(F32), axis=0, keepdims=True)
    sums_ref[...] = sums
    rows_copy.wait()
    weight_grad = jnp.transpose(dot(result, rows_ref[...], 0, 0))
    out_weight_grad = jnp.transpose(dot(out, grad_ref[...], 0, 0))
    high = sums.astype(BF16)
    low = (sums - high.astype(F32)).astype(BF16)
    weight = weight_ref[...]
    shift = dot(high, weight, 1, 1) + dot(low, weight, 1, 1)
    gain = (to_row(weight.astype(F32) * weight_grad) - norm_ref[1:2, :] * shift) / norm_ref[0:1, :]
    vector_ref[0:1, :] = gain
    vector_ref[1:2, :] = shift
    wide = weight_grad.shape[1]
    if kind == "flat":
        whole_ref = refs[ties + 4]
        whole_ref[:, :wide] = weight_grad
        whole_ref[:, wide:] = out_weight_grad
        return
    target = refs[ties + 4] if kind == "whole" else product_ref
    count, shard = target.shape[:2]
    target[:, :, :wide] = weight_grad.reshape(count, shard, wide)
    target[:, :, wide:] = out_weight_grad.reshape(count, shard, PAIR)
    if kind == "whole":
        return
    kept_ref, away_ref = refs[ties + 4 : ties + 6]
    for block in range(count // 2):
        keep = scatter_block(info_ref, 0, block, False, count)
        send = scatter_block(info_ref, 0, block, True, count)
        start = 0
        if kind == "joined":
            start = before_ref.shape[2]
            kept_ref[block, :, :start] = before_ref[keep]
            away_ref[block, :, :start] = before_ref[send].astype(BF16)
        kept_ref[block, :, start:] = product_ref[keep]
        away_ref[block, :, start:] = product_ref[send].astype(BF16)


def feed_forward_kernel(
    info_ref,
    own_ref,
    other_ref,
    cot_own_ref,
    cot_other_ref,
    bias_ref,
    *refs,
    blocks,
    placed,
):
    weights, refs = refs[:2], refs[2:]
    terms_own_ref, terms_other_ref, back_own_ref, back_other_ref, sums_ref = refs[:5]
    refs = refs[5:]
    step = pl.program_id(0)
    own = step < blocks
    if placed:
        grad_fc_ref, grad_proj_ref = refs
        fc, proj = (ref[...] for ref in weights)
    else:
        kept_ref, away_ref, fc_ref, proj_ref, grad_fc_ref, grad_proj_ref, away_scratch, sems = refs
        count = fc_ref.shape[0]
        half = count // 2

        @pl.when(step == 0)
        def _():
            copies = []
            for number, target in enumerate((fc_ref, proj_ref)):
                for place in range(count):
                    source = weights[place // half].at[
                        place % half, :, pl.ds(number * target.shape[2], target.shape[2])
                    ]
                    copies.append(
                        pltpu.make_async_copy(
                            source,
                            target.at[gathered_owner(info_ref, place, count)],
                            sems.at[number * count + place],
                        )
                    )
                    copies[-1].start()
            for copy in copies:
                copy.wait()

        fc, proj = (ref[...].reshape(-1, ref.shape[2]) for ref in (fc_ref, proj_ref))

    @pl.when(step == 0)
    def _():
        sums_ref[...] = jnp.zeros_like(sums_ref)
        grad_fc_ref[...] = jnp.zeros_like(grad_fc_ref)
        grad_proj_ref[...] = jnp.zeros_like(grad_proj_ref)

    rows = jnp.where(own, own_ref[...], other_ref[...])
    cot = jnp.where(own, cot_own_ref[...], cot_other_ref[...])
    pre = dot(rows, fc) + bias_ref[...]
    slope = math.sqrt(2.0 / math.pi)
    square = pre * pre
    bent = jnp.tanh(slope * pre * (1.0 + 0.044715 * square))
    upper = 0.5 * (1.0 + bent)
    act = (pre * upper).astype(BF16)
    terms = dot(act, proj, 1, 1)
    grad_proj_ref[...] += dot(cot, act, 0, 0).reshape(grad_proj_ref.shape)
    derivative = upper + 0.5 * pre * (1.0 - bent * bent) * (
        slope * (1.0 + 3.0 * 0.044715 * square)
    )
    grad_pre = (dot(cot, proj) * derivative).astype(BF16)
    back = dot(grad_pre, fc, 1, 1)
    grad_fc_ref[...] += dot(rows, grad_pre, 0, 0).reshape(grad_fc_ref.shape)
    sums_ref[...] += jnp.sum(grad_pre.astype(F32), axis=0, keepdims=True)

    @pl.when(own)
    def _():
        terms_own_ref[...] = terms
        back_own_ref[...] = back

    @pl.when(jnp.logical_not(own))
    def _():
        terms_other_ref[...] = terms.astype(BF16)
        back_other_ref[...] = back.astype(BF16)

    if not placed:
        hidden = fc_ref.shape[2]

        @pl.when(step == 2 * blocks - 1)
        def _():
            copies = []
            for number, grad_ref in enumerate((grad_fc_ref, grad_proj_ref)):
                for block in range(half):
                    copies.append(
                        pltpu.make_async_copy(
                            grad_ref.at[scatter_block(info_ref, 0, block, False, count)],
                            kept_ref.at[block, :, pl.ds(number * hidden, hidden)],
                            sems.at[number * half + block],
                        )
                    )
                    copies[-1].start()
            for number, grad_ref in enumerate((grad_fc_ref, grad_proj_ref)):
                for block in range(half):
                    away_scratch[block, :, number * hidden : (number + 1) * hidden] = grad_ref[
                        scatter_block(info_ref, 0, block, True, count)
                    ].astype(BF16)
            send = pltpu.make_async_copy(away_scratch, away_ref, sems.at[2 * half])
            send.start()
            for copy in copies + [send]:
                copy.wait()


ANY_SPEC = pl.BlockSpec(memory_space=pl.ANY)
TOKEN_SHAPE = jax.ShapeDtypeStruct((1, 1), F32)
TOKEN_SPEC = pl.BlockSpec((1, 1), lambda *_: (0, 0))


def attend_forward(pair, normed, weight, bias, ties):
    halves = isinstance(normed, tuple)
    tokens = 2 * normed[1].shape[0] if halves else normed.shape[0]
    features, columns = weight.shape
    every = pl.BlockSpec((tokens, features), lambda: (0, 0))
    in_specs = [
        pl.BlockSpec((features, columns), lambda: (0, 0)),
        pl.BlockSpec((1, columns), lambda: (0, 0)),
    ]
    out_specs = [
        pl.BlockSpec((tokens, columns), lambda: (0, 0)),
        pl.BlockSpec((tokens, PAIR), lambda: (0, 0)),
        pl.BlockSpec((2, tokens), lambda: (0, 0)),
        pl.BlockSpec((1, 1), lambda: (0, 0)),
    ]
    out_shape = [
        jax.ShapeDtypeStruct((tokens, columns), BF16),
        jax.ShapeDtypeStruct((tokens, PAIR), BF16),
        jax.ShapeDtypeStruct((2, tokens), F32),
        TOKEN_SHAPE,
    ]
    if halves:
        half = pl.BlockSpec((tokens // 2, features), lambda: (0, 0))
        in_specs += [pl.BlockSpec(memory_space=pltpu.SMEM), half, half]
        out_specs = [every] + out_specs
        out_shape = [jax.ShapeDtypeStruct((tokens, features), BF16)] + out_shape
    else:
        in_specs += [every]
    in_specs += [ANY_SPEC] * len(ties)
    out = pl.pallas_call(
        functools.partial(forward_kernel, rows=512, halves=halves),
        in_specs=in_specs,
        out_specs=out_specs,
        out_shape=out_shape,
        compiler_params=pltpu.CompilerParams(vmem_limit_bytes=VMEM_BYTES),
        cost_estimate=SMALL_COST,
        name=f"attend_forward_{pair}",
    )(weight, bias, *(normed if halves else (normed,)), *ties)
    return out[0] if halves else normed, *out[-4:-1], out[-1].reshape(())


def attend_backward(
    pair, kind, projected, heads, lse, weight, info, own, other, normed, out_weight, norm, ties
):
    tokens, columns = projected.shape
    features = normed.shape[1]
    count = lax.axis_size("dp")
    shard = features // count
    fixed = lambda shape: pl.BlockSpec(shape, lambda _: (0,) * len(shape))
    scalars = pl.BlockSpec(memory_space=pltpu.SMEM)
    out_shape = [
        jax.ShapeDtypeStruct((tokens, columns), BF16),
        jax.ShapeDtypeStruct((1, columns), F32),
        jax.ShapeDtypeStruct((2, features), F32),
        TOKEN_SHAPE,
    ]
    wide = 4 * PAIR
    product = pltpu.VMEM((8, 128), F32)
    tie_specs = [ANY_SPEC] * len(ties)
    if shard % 16:
        inner = "flat"
        out_shape += [jax.ShapeDtypeStruct((features, wide), F32)]
    elif kind == "whole":
        inner = kind
        out_shape += [jax.ShapeDtypeStruct((count, shard, wide), F32)]
    else:
        inner = kind
        width = wide
        if kind == "joined":
            width += ties[0].shape[2]
            tie_specs[0] = fixed(ties[0].shape)
        out_shape += [
            jax.ShapeDtypeStruct((count // 2, shard, width), held) for held in (F32, BF16)
        ]
        product = pltpu.VMEM((count, shard, wide), F32)
    out = pl.pallas_call(
        functools.partial(backward_kernel, rows=256, ties=len(ties), kind=inner),
        grid=(1,),
        in_specs=[
            scalars,
            fixed(projected.shape),
            fixed(heads.shape),
            fixed(lse.shape),
            ANY_SPEC,
            ANY_SPEC,
            ANY_SPEC,
            fixed(weight.shape),
            pl.BlockSpec((features, PAIR), lambda _: (0, pair)),
            fixed(norm.shape),
        ]
        + tie_specs,
        out_specs=[fixed(result.shape) for result in out_shape],
        out_shape=out_shape,
        scratch_shapes=[
            pltpu.VMEM((tokens, features), BF16),
            pltpu.VMEM((PAIR, tokens), F32),
            product,
            pltpu.VMEM((tokens, features), BF16),
            pltpu.SemaphoreType.DMA((3,)),
        ],
        compiler_params=pltpu.CompilerParams(vmem_limit_bytes=VMEM_BYTES),
        cost_estimate=SMALL_COST,
        name=f"attend_backward_{pair}",
    )(info, projected, heads, lse, own, other, normed, weight, out_weight, norm, *ties)
    if kind == "whole":
        gradient = out[4]
    elif shard % 16:
        gradient = Scatter(out[4] if kind == "split" else jnp.concatenate([ties[0], out[4]], axis=1))
    else:
        gradient = Scatter(out[4], out[5])
    return out[0], out[1], out[2], out[3], gradient


def feed_forward(info, own, other, cot_own, cot_other, bias, gather):
    tokens, features = own.shape
    hidden = bias.shape[0]
    block = 512
    blocks = tokens // block
    count = lax.axis_size("dp")
    shard = features // count
    placed = shard % 16 != 0
    first = pl.BlockSpec((block, features), lambda i: (jnp.minimum(i, blocks - 1), 0))
    second = pl.BlockSpec((block, features), lambda i: (jnp.maximum(i - blocks, 0), 0))
    out_specs = [first, second, first, second, pl.BlockSpec((1, hidden), lambda i: (0, 0))]
    out_shape = [
        jax.ShapeDtypeStruct((tokens, features), kind) for kind in (F32, BF16, F32, BF16)
    ] + [jax.ShapeDtypeStruct((1, hidden), F32)]
    scratch = []
    weights = [gather.held, gather.got]
    weight_specs = [ANY_SPEC] * 2
    if placed:
        both = gather.result()
        weights = [both[:, :hidden], both[:, hidden:]]
        weight_specs = [pl.BlockSpec((features, hidden), lambda i: (0, 0))] * 2
        out_specs += [pl.BlockSpec((features, hidden), lambda i: (0, 0))] * 2
        out_shape += [jax.ShapeDtypeStruct((features, hidden), F32)] * 2
    else:
        out_specs += [ANY_SPEC] * 2
        out_shape += [
            jax.ShapeDtypeStruct((count // 2, shard, 2 * hidden), kind) for kind in (F32, BF16)
        ]
        scratch = [
            pltpu.VMEM((count, shard, hidden), BF16),
            pltpu.VMEM((count, shard, hidden), BF16),
            pltpu.VMEM((count, shard, hidden), F32),
            pltpu.VMEM((count, shard, hidden), F32),
            pltpu.VMEM((count // 2, shard, 2 * hidden), BF16),
            pltpu.SemaphoreType.DMA((2 * count,)),
        ]
    out = pl.pallas_call(
        functools.partial(feed_forward_kernel, blocks=blocks, placed=placed),
        grid=(2 * blocks,),
        in_specs=[
            pl.BlockSpec(memory_space=pltpu.SMEM),
            first,
            second,
            first,
            second,
            pl.BlockSpec((1, hidden), lambda i: (0, 0)),
        ]
        + weight_specs,
        out_specs=out_specs,
        out_shape=out_shape,
        scratch_shapes=scratch,
        compiler_params=pltpu.CompilerParams(vmem_limit_bytes=VMEM_BYTES),
        cost_estimate=SMALL_COST,
        name="feed_forward",
    )(info, own, other, cot_own, cot_other, bias.reshape(1, hidden), *weights)
    if placed:
        return (*out[:5], Scatter(jnp.concatenate(out[5:], axis=1)))
    return (*out[:5], Scatter(*out[5:]))


def block_call(kernel, grid, in_specs, operands, out, scratch=(), name=None, ties=()):
    return pl.pallas_call(
        kernel,
        grid=grid,
        in_specs=list(in_specs) + [ANY_SPEC] * len(ties),
        out_specs=[pl.BlockSpec(block, index) for _, _, block, index in out],
        out_shape=[jax.ShapeDtypeStruct(shape, kind) for shape, kind, _, _ in out],
        scratch_shapes=list(scratch),
        compiler_params=pltpu.CompilerParams(vmem_limit_bytes=VMEM_BYTES),
        cost_estimate=SMALL_COST,
        name=name,
    )(*operands, *ties)


def whole_spec(array):
    return pl.BlockSpec(array.shape, lambda *_: (0,) * array.ndim)


def out_product_kernel(info_ref, weight_ref, *refs):
    heads_refs, (own_ref, other_ref) = refs[:-2], refs[-2:]
    half = own_ref.shape[0]
    for target, at in ((other_ref, 1 - info_ref[1]), (own_ref, info_ref[1])):
        here = pl.ds(pl.multiple_of(at * half, half), half)
        heads = jnp.concatenate([ref[here, :] for ref in heads_refs], axis=1)
        target[...] = dot(heads, weight_ref[...], 1, 1).astype(target.dtype)


def out_product(info, weight, heads):
    half = heads[0].shape[0] // 2
    width = weight.shape[0]
    return block_call(
        out_product_kernel,
        (1,),
        [pl.BlockSpec(memory_space=pltpu.SMEM), whole_spec(weight)] + [whole_spec(h) for h in heads],
        [info, weight, *heads],
        [((half, width), kind, (half, width), lambda _: (0, 0)) for kind in (F32, BF16)],
        name="out_product",
    )


def back_product_kernel(info_ref, *refs, pairs):
    own_ref, other_ref = refs[-2:]
    half = own_ref.shape[0]
    for target, at in ((other_ref, 1 - info_ref[1]), (own_ref, info_ref[1])):
        here = pl.ds(pl.multiple_of(at * half, half), half)
        total = 0.0
        for result, weight in zip(refs[:pairs], refs[pairs : 2 * pairs]):
            total = total + dot(result[here, :], weight[...], 1, 1)
        target[...] = total.astype(target.dtype)


def back_product(info, results, weights, ties):
    half = results[0].shape[0] // 2
    width = weights[0].shape[0]
    return block_call(
        functools.partial(back_product_kernel, pairs=len(results)),
        (1,),
        [pl.BlockSpec(memory_space=pltpu.SMEM)] + [whole_spec(a) for a in (*results, *weights)],
        [info, *results, *weights],
        [((half, width), kind, (half, width), lambda _: (0, 0)) for kind in (F32, BF16)],
        name="back_product",
        ties=ties,
    )


def middle_kernel(hidden_ref, own_ref, other_ref, bias_ref, norm_ref, *refs):
    middle_ref, normed_ref = refs[-2:]
    middle = (
        hidden_ref[...].astype(F32) + (own_ref[...] + other_ref[...].astype(F32)) + bias_ref[...]
    )
    middle_ref[...] = middle
    normed_ref[...] = norm_layer(middle, norm_ref[0:1, :], norm_ref[1:2, :]).astype(BF16)


def middle_norm(hidden, own, other, bias, norm, ties):
    rows, width = hidden.shape
    tile = pl.BlockSpec((256, width), lambda i: (i, 0))
    return block_call(
        middle_kernel,
        (rows // 256,),
        [tile, tile, tile, whole_spec(bias), whole_spec(norm)],
        [hidden, own, other, bias, norm],
        [(hidden.shape, kind, (256, width), lambda i: (i, 0)) for kind in (F32, BF16)],
        name="middle_norm",
        ties=ties,
    )


def norm_slope(rows, grad, gain):
    centred = rows - jnp.mean(rows, axis=-1, keepdims=True)
    scale = lax.rsqrt(jnp.mean(centred * centred, axis=-1, keepdims=True) + 1e-05)
    normalised = centred * scale
    scaled = grad * gain
    back = scale * (
        scaled
        - jnp.mean(scaled, axis=-1, keepdims=True)
        - normalised * jnp.mean(scaled * normalised, axis=-1, keepdims=True)
    )
    return normalised, back


def middle_back_kernel(
    middle_ref, own_ref, other_ref, cot_ref, norm_ref, grad_ref, attn_ref, sums_ref
):
    @pl.when(pl.program_id(0) == 0)
    def _():
        sums_ref[...] = jnp.zeros_like(sums_ref)

    back = own_ref[...] + other_ref[...].astype(F32)
    cot = cot_ref[...].astype(F32)
    normalised, through = norm_slope(middle_ref[...], back, norm_ref[0:1, :])
    grad = cot + through
    attn = grad.astype(BF16)
    grad_ref[...] = grad
    attn_ref[...] = attn
    for row, values in enumerate((back * normalised, back, attn.astype(F32), cot)):
        sums_ref[row : row + 1, :] += jnp.sum(values, axis=0, keepdims=True)


def middle_back(middle, own, other, cot, norm):
    rows, width = middle.shape
    tile = pl.BlockSpec((256, width), lambda i: (i, 0))
    return block_call(
        middle_back_kernel,
        (rows // 256,),
        [tile, tile, tile, tile, whole_spec(norm)],
        [middle, own, other, cot, norm],
        [(middle.shape, kind, (256, width), lambda i: (i, 0)) for kind in (F32, BF16)]
        + [((8, width), F32, (8, width), lambda i: (0, 0))],
        name="middle_back",
    )


def first_back_kernel(hidden_ref, own_ref, other_ref, grad_ref, norm_ref, *refs):
    result_ref = refs[-1]
    back = own_ref[...] + other_ref[...].astype(F32)
    _, through = norm_slope(hidden_ref[...].astype(F32), back, norm_ref[0:1, :])
    result_ref[...] = (grad_ref[...] + through).astype(BF16)


def first_back(hidden, own, other, grad, norm, ties):
    rows, width = hidden.shape
    tile = pl.BlockSpec((256, width), lambda i: (i, 0))
    return block_call(
        first_back_kernel,
        (rows // 256,),
        [tile, tile, tile, tile, whole_spec(norm)],
        [hidden, own, other, grad, norm],
        [(hidden.shape, BF16, (256, width), lambda i: (i, 0))],
        name="first_back",
        ties=ties,
    )[0]


def vectors_kernel(early_ref, hidden_ref, *refs, pairs):
    out_ref = refs[-1]
    width = out_ref.shape[1]
    out_ref[...] = jnp.zeros_like(out_ref)
    out_ref[0:2, :] = sum(ref[...] for ref in refs[:pairs])
    out_ref[2:6, :] = early_ref[0:4, :]
    wide = hidden_ref.shape[1] // width
    for row in range(wide):
        out_ref[6 + row : 7 + row, :] = hidden_ref[:, row * width : (row + 1) * width]
    for pair, ref in enumerate(refs[pairs : 2 * pairs]):
        start = pair * PAIR
        out_ref[6 + wide : 7 + wide, start : start + PAIR] = ref[:, :PAIR]
        start += pairs * PAIR
        out_ref[6 + wide : 7 + wide, start : start + PAIR] = ref[:, 2 * PAIR :]


def vectors_of(early, hidden, parts, sums, ties):
    operands = [early, hidden, *parts, *sums]
    return block_call(
        functools.partial(vectors_kernel, pairs=len(parts)),
        (1,),
        [whole_spec(a) for a in operands],
        operands,
        [((16, early.shape[1]), F32, (16, early.shape[1]), lambda _: (0, 0))],
        name="vectors",
        ties=ties,
    )[0]


def join_gathered_kernel(token_ref, held_ref, got_ref, *refs):
    @pl.when(pl.program_id(0) == 0)
    def _():
        refs[-1][...] = held_ref[...]

    @pl.when(pl.program_id(0) == 1)
    def _():
        refs[-1][...] = got_ref[...]


def join_gathered(held, got, token, ties):
    if held.shape[1] % 16 or token is None:
        return jnp.concatenate([held, got], axis=0)
    count, rows, columns = held.shape
    token = token.reshape(1, 1)
    return block_call(
        join_gathered_kernel,
        (2,),
        [pl.BlockSpec(memory_space=pltpu.SMEM), whole_spec(held), whole_spec(got)],
        [token, held, got],
        [((2 * count, rows, columns), held.dtype, held.shape, lambda i: (i, 0, 0))],
        name="join_gathered",
        ties=ties,
    )[0]


def exchange(block, bits):
    count = lax.axis_size("dp")
    width = lax.axis_size("tensor")
    pairs = [
        (i * width + t, (i ^ (1 << bits[t % 2])) * width + t)
        for i in range(count)
        for t in range(width)
    ]
    return lax.ppermute(block, ("dp", "tensor"), pairs)


def swap(block):
    count = lax.axis_size("tensor")
    return lax.ppermute(block, "tensor", [(i, count - 1 - i) for i in range(count)])


class Gather:
    def __init__(self, shard):
        self.orders = list(zip(*gather_orders(lax.axis_size("dp"))))
        self.held = shard[None]
        self.step = 0
        self.got = exchange(self.held, self.orders[0])

    def advance(self, token=None, ties=()):
        self.step += 1
        if self.step < len(self.orders):
            self.held = join_gathered(self.held, self.got, token, ties)
            self.got = exchange(self.held, self.orders[self.step])
        return self

    def result(self, token=None):
        while self.step < len(self.orders) - 1:
            self.advance()
        return place_rows(place_info(), self.held, self.got, token)


def place_kernel(info_ref, token_ref, held_ref, got_ref, out_ref, sems):
    half = held_ref.shape[0]
    copies = []
    for place in range(2 * half):
        source = held_ref.at[place] if place < half else got_ref.at[place - half]
        owner = gathered_owner(info_ref, place, 2 * half)
        copies.append(pltpu.make_async_copy(source, out_ref.at[owner], sems.at[place]))
        copies[-1].start()
    for copy in copies:
        copy.wait()


def place_rows(info, held, got, token=None):
    half, rows, columns = held.shape
    count = 2 * half
    if rows % 16:
        owners = gathered_owner(info, jnp.arange(count, dtype=jnp.int32), count)
        placed = jnp.concatenate([held, got], axis=0)[jnp.argsort(owners)]
        return placed.reshape(count * rows, columns)
    placed = pl.pallas_call(
        place_kernel,
        in_specs=[pl.BlockSpec(memory_space=pltpu.SMEM)] * 2 + [ANY_SPEC] * 2,
        out_specs=pl.BlockSpec(memory_space=pltpu.VMEM),
        out_shape=jax.ShapeDtypeStruct((count, rows, columns), BF16),
        scratch_shapes=[pltpu.SemaphoreType.DMA((count,))],
        compiler_params=pltpu.CompilerParams(vmem_limit_bytes=16 * 1024 * 1024),
        cost_estimate=SMALL_COST,
        name="place_rows",
    )(info, jnp.zeros((1, 1), F32) if token is None else token.reshape(1, 1), held, got)
    return placed.reshape(count * rows, columns)


def join_kernel(info_ref, token_ref, keep_ref, send_ref, got_keep_ref, got_send_ref, *refs):
    kept_ref, away_ref = refs[-2:]
    kept_ref[...] = keep_ref[...] + got_keep_ref[...].astype(F32)
    away_ref[...] = (send_ref[...] + got_send_ref[...].astype(F32)).astype(BF16)


def join_halves(info, step, held, got, token, ties):
    count, rows, columns = held.shape
    half = count // 2
    size = lax.axis_size("dp")

    def at(sent):
        return pl.BlockSpec(
            (1, rows, columns), lambda i, info: (scatter_block(info, step, i, sent, size), 0, 0)
        )

    result = pl.BlockSpec((1, rows, columns), lambda i, info: (i, 0, 0))
    return pl.pallas_call(
        join_kernel,
        grid_spec=pltpu.PrefetchScalarGridSpec(
            num_scalar_prefetch=1,
            grid=(half,),
            in_specs=[pl.BlockSpec(memory_space=pltpu.SMEM), at(False), at(True), at(False), at(True)]
            + [ANY_SPEC] * len(ties),
            out_specs=[result, result],
        ),
        out_shape=[jax.ShapeDtypeStruct((half, rows, columns), kind) for kind in (F32, BF16)],
        compiler_params=pltpu.CompilerParams(vmem_limit_bytes=16 * 1024 * 1024),
        cost_estimate=SMALL_COST,
        name="join_halves",
    )(info, jnp.zeros((1, 1), F32) if token is None else token, held, held, got, got, *ties)


class Scatter:
    def __init__(self, whole, away=None):
        self.orders = list(zip(*scatter_orders(lax.axis_size("dp"))))
        self.step = 0
        if away is None:
            count = lax.axis_size("dp")
            self.split(whole.reshape(count, whole.shape[0] // count, whole.shape[1]))
        else:
            self.kept, self.away = whole, away
        self.got = exchange(self.away, self.orders[0])

    def split(self, held):
        count = lax.axis_size("dp")
        blocks = jnp.arange(held.shape[0] // 2, dtype=jnp.int32)
        keep, send = (
            scatter_block(place_info(), self.step, blocks, sent, count) for sent in (False, True)
        )
        self.kept = jnp.take(held, keep, axis=0)
        self.away = jnp.take(held, send, axis=0).astype(BF16)

    def advance(self, token=None, ties=()):
        self.step += 1
        if self.kept.shape[1] % 16:
            self.split(self.kept + self.got.astype(F32))
        else:
            self.kept, self.away = join_halves(
                place_info(), self.step, self.kept, self.got, token, ties
            )
        self.got = exchange(self.away, self.orders[self.step])

    def result(self):
        while self.step < len(self.orders) - 1:
            self.advance()
        return (self.kept + self.got.astype(F32))[0]


class VectorSum:
    def __init__(self, rows, both):
        self.rows, self.both, self.bit = rows, both, 0

    def advance(self, steps=1):
        for _ in range(steps):
            if self.bit < bits_of(lax.axis_size("dp")):
                self.rows = self.rows + exchange(self.rows, (self.bit, self.bit))
                self.bit += 1
        return self.rows

    def result(self):
        self.advance(bits_of(lax.axis_size("dp")))
        return self.rows[: self.both] + swap(self.rows[: self.both]), self.rows[self.both :]


def per_device(
    hidden_in,
    first_gain,
    first_shift,
    qkv_weight,
    qv_bias,
    out_weight,
    out_bias,
    second_gain,
    second_shift,
    fc_weight,
    fc_bias,
    proj_weight,
    proj_bias,
    cotangent,
):
    width = hidden_in.shape[1]
    shard_rows = qkv_weight.shape[0]
    head_width = qkv_weight.shape[2]
    pairs = head_width // PAIR
    columns = 3 * PAIR

    by_pair = qkv_weight.reshape(shard_rows, 3, pairs, PAIR).swapaxes(1, 2)
    by_pair = by_pair.reshape(shard_rows, pairs * columns)
    early = pairs - 1
    first_gather = Gather(by_pair[:, : early * columns])
    rest_gather = Gather(jnp.concatenate([by_pair[:, early * columns :], out_weight], axis=1))
    ff_gather = Gather(jnp.concatenate([fc_weight, proj_weight], axis=1))

    rows_first = hidden_in.astype(F32)
    row_mean = jnp.mean(rows_first, axis=-1, keepdims=True)
    centred = rows_first - row_mean
    first_rsqrt = lax.rsqrt(jnp.mean(centred * centred, axis=-1, keepdims=True) + 1e-05)
    normed_piece = (centred * first_rsqrt * first_gain + first_shift).astype(BF16)
    info = place_info()
    normed_first = (info, normed_piece, swap(normed_piece))
    cot_other = swap(cotangent)

    bias_parts = jnp.stack([qv_bias[0], jnp.zeros_like(qv_bias[0]), qv_bias[1]])
    bias_cols = bias_parts.reshape(3, pairs, PAIR).swapaxes(0, 1).reshape(pairs, 1, columns)
    ff_gather.advance()
    for _ in range(len(rest_gather.orders) - 1):
        rest_gather.advance()
    weights = first_gather.result()
    qkv_weights = [weights[:, p * columns : (p + 1) * columns] for p in range(early)]
    projected, heads, lses = [], [], []
    for pair in range(pairs):
        normed_first, columns_out, heads_out, lse, token = attend_forward(
            pair,
            normed_first,
            qkv_weights[pair],
            bias_cols[pair],
            [ff_gather.held] if pair else [rest_gather.held],
        )
        projected.append(columns_out)
        heads.append(heads_out)
        lses.append(lse)
        if pair == early - 1:
            rest = rest_gather.result(token)
            qkv_weights.append(rest[:, :columns])
            full_out = rest[:, columns:]
        if pair < pairs - 1:
            ff_gather.advance(token)

    attn_own, attn_other = out_product(info, full_out, heads)
    norm_second = jnp.stack([second_gain, second_shift])
    middle, normed_own = middle_norm(
        hidden_in,
        attn_own,
        swap(attn_other),
        out_bias[None],
        norm_second,
        [ff_gather.got],
    )
    normed_other = swap(normed_own)
    terms_own, terms_other, back_own, back_other, sum_fc, ff_sum = feed_forward(
        info, normed_own, normed_other, cotangent, cot_other, fc_bias, ff_gather
    )
    back_other = swap(back_other)
    terms_other = swap(terms_other)
    block_out = (middle + (terms_own + terms_other.astype(F32)) + proj_bias).astype(BF16)
    grad_middle, grad_attn, sums_second = middle_back(
        middle, back_own, back_other, cotangent, norm_second
    )
    grad_attn_other = swap(grad_attn)
    hidden = fc_weight.shape[1]
    norm_first = jnp.stack([first_gain, first_shift])
    shared = (info, grad_attn, grad_attn_other, normed_first, full_out, norm_first)
    kinds = ["split"] + ["whole"] * (pairs - 2) + ["joined"]
    results, column_sums, vector_parts = [], [], []
    first_sum = rest_sum = whole = None
    for pair in range(pairs):
        ties = [] if whole is None else [whole]
        if pair:
            ties += [ff_sum.away, first_sum.away]
        result, sums, vector, token, gradient = attend_backward(
            pair,
            kinds[pair],
            projected[pair],
            heads[pair],
            lses[pair],
            qkv_weights[pair],
            *shared,
            ties,
        )
        results.append(result)
        column_sums.append(sums)
        vector_parts.append(vector)
        if pair < pairs - 1:
            ff_sum.advance(token)
            if pair:
                first_sum.advance(token)
        if pair == 0:
            first_sum = gradient
        elif pair == pairs - 1:
            rest_sum = gradient
        else:
            whole = gradient
    back_own, back_other = back_product(info, results, qkv_weights, [])
    ff_sum.advance(ties=(back_other,))
    first_sum.advance(ties=(back_other,))
    rest_sum.advance(ties=(ff_sum.away, first_sum.away))
    grad_hidden = first_back(
        hidden_in, back_own, swap(back_other), grad_middle, norm_first, [rest_sum.away]
    )
    vector_sum = VectorSum(
        vectors_of(sums_second, sum_fc, vector_parts, column_sums, [rest_sum.away]), 6
    )
    first_sum.advance(ties=(rest_sum.away,))
    rest_sum.advance(ties=(first_sum.away, vector_sum.advance()))
    rest_sum.advance(ties=(vector_sum.advance(2), grad_hidden))
    own_heads = jnp.concatenate([first_sum.result(), rest_sum.result()], axis=1).reshape(
        shard_rows, pairs, 4, PAIR
    )
    own_outw = own_heads[:, :, 3].reshape(shard_rows, head_width)
    own_qkv = own_heads[:, :, :3].swapaxes(1, 2).reshape(shard_rows, 3, head_width)
    own_ff = ff_sum.result()
    sums, own_sums = vector_sum.result()
    hidden_rows = hidden // width
    return (
        block_out,
        grad_hidden,
        sums[0],
        sums[1],
        own_qkv,
        own_sums[hidden_rows].reshape(2, head_width),
        own_outw,
        sums[4],
        sums[2],
        sums[3],
        own_ff[:, :hidden],
        own_sums[:hidden_rows].reshape(hidden),
        own_ff[:, hidden:],
        sums[5],
    )


def solution(mesh):
    placed = (
        P(("dp", "tensor"), None),
        P(),
        P(),
        P("dp", None, "tensor"),
        P(None, "tensor"),
        P("dp", "tensor"),
        P(),
        P(),
        P(),
        P("dp", "tensor"),
        P("tensor"),
        P("dp", "tensor"),
        P(),
        P(("dp", "tensor"), None),
    )
    return jax.shard_map(
        per_device,
        mesh=mesh,
        in_specs=placed,
        out_specs=(
            P(("dp", "tensor"), None),
            P(("dp", "tensor"), None),
            P(),
            P(),
            P("dp", None, "tensor"),
            P(None, "tensor"),
            P("dp", "tensor"),
            P(),
            P(),
            P(),
            P("dp", "tensor"),
            P("tensor"),
            P("dp", "tensor"),
            P(),
        ),
        check_vma=False,
    )
```
